256 devices in a mesh: tile: 32 (over x, z), lev: 8 (over y, core).
Axes of the slice: x: 4, y: 4, z: 8, core: 2. Of those that a mesh axis runs over, the one named last changes fastest.
Arguments:
- tracers: bfloat16 [8192, 4, 64, 128], P('tile', None, 'lev'), may hold values from -6 to 6
- sweeps: bfloat16 [2, 16, 128, 128], replicated, may hold values from -0.2 to 1.2
- targets: int32 [8192, 3], P('tile'), may hold values from 0 to 8191, as said below
- matrix_ids: int32 [8192, 3, 2], P('tile'), may hold values from 0 to 15
- self_ids: int32 [8192, 2], P('tile'), may hold values from 0 to 15
- vertical: float32 [9, 64, 8192], P(None, 'lev', 'tile'), may hold values from -1 to 1
Outputs:
- remapped: bfloat16 [8192, 4, 64, 128], P('tile', None, 'lev')
The draws below stay inside these ranges and needn't reach their ends.
Inputs may be any that keep to these rules, and one draw needn't show every extreme that they name: `targets`: let the owner of a target be target // 256. There is one hot tile index and one other cold tile index, the same for all sources: the 3 partials of the 256 blocks of every tile index go exactly 48 times to the hot one, never to the cold one, and exactly 24 times to each other tile index.
All inputs are finite; a program needn't handle non-finite values.
Results may differ from the reference program's by a relative error of at most 0.0063.
Values may be sent and summed in bfloat16 or wider, within the bound.
A program may use at most 192 MiB of HBM per device.

```python
import math
import jax
import jax.numpy as jnp
from jax import lax

BS = 128
TRACERS = 4
REACH = 4
PAIRS = 3
MATS = 16
BLOCKS_DEV = 256
BLOCKS = 8192
LEVELS = 64
MEAN = 24
CAP = 48
N_TILE = 32


def draw_sweeps(key, part):
    key = jax.random.fold_in(key, 21)
    identity = (jnp.arange(BS)[:, None] == jnp.arange(BS)[None, :]).astype(jnp.float32)
    noise = 0.4 * jax.random.normal(key, (2, MATS, BS, BS), jnp.float32) / math.sqrt(BS)
    noise = jnp.clip(noise, -0.2, 0.2)
    return (identity[None, None] + noise).astype(jnp.bfloat16)


def draw_targets(key, part):
    key = jax.random.fold_in(key, 11)
    pair_total = BLOCKS_DEV * PAIRS
    hot_tile = jax.random.randint(jax.random.fold_in(key, 1), (), 0, N_TILE)
    cold_tile = (hot_tile + 1 + jax.random.randint(jax.random.fold_in(key, 4), (), 0, N_TILE - 1)) % N_TILE
    every_tile = jnp.arange(N_TILE, dtype=jnp.int32)
    drawn = jnp.logical_and(every_tile != hot_tile, every_tile != cold_tile)
    ranked = jnp.argsort(jnp.where(drawn, 0, 1) * N_TILE + every_tile).astype(jnp.int32)
    pool = ranked[jnp.arange((N_TILE - 2) * MEAN, dtype=jnp.int32) // MEAN]

    def one_source(source_key):
        owners = jnp.concatenate([jnp.full((CAP,), hot_tile, jnp.int32), pool])
        return jax.random.permutation(source_key, owners)
    source_keys = jax.random.split(jax.random.fold_in(key, 2), N_TILE)
    owners = jax.vmap(one_source)(source_keys)
    local_block = jax.random.randint(jax.random.fold_in(key, 3), (N_TILE, pair_total), 0, BLOCKS_DEV)
    return (owners * BLOCKS_DEV + local_block).reshape(BLOCKS, PAIRS).astype(jnp.int32)


def touch_ends(drawn, stream_key, smallest, top_value):
    extent = drawn.shape
    place = [jax.random.randint(jax.random.fold_in(stream_key, axis), (), 0, extent[axis]) for axis in range(len(extent))]
    drawn = drawn.at[tuple(place)].set(smallest)
    longest = extent.index(max(extent))
    place[longest] = (place[longest] + 1) % extent[longest]
    return drawn.at[tuple(place)].set(top_value)


def steps_of(stream_key, dims, pieces, smallest, largest):
    def one(dim, shards_of):
        steps = jax.random.uniform(jax.random.fold_in(jax.random.fold_in(stream_key, 6), dim), (shards_of,), jnp.float32, smallest / len(pieces), largest / len(pieces))
        return jnp.repeat(jnp.exp(steps), dims[dim] // shards_of).reshape((-1,) + (1,) * (len(dims) - dim - 1))

    loudness = one(*pieces[0])
    for cut in pieces[1:]:
        loudness = loudness * one(*cut)
    return loudness


def bell_draw(rng, dims, spread, most, pieces=(), kind=jnp.bfloat16):
    loudness = steps_of(rng, dims, pieces, -0.22, 0.18) if pieces else 1.0
    entries = jax.random.normal(rng, dims, jnp.float32) * spread * loudness
    return jnp.minimum(jnp.maximum(entries, -most), most).astype(kind)


def setup_inputs(seed: int = 0) -> dict:
    key_of = jax.random.split(jax.random.key(seed), 7)
    tracers = bell_draw(key_of[0], (BLOCKS, TRACERS, LEVELS, BS), 1.0, 6.0, ((0, 32), (2, 8)))
    sweeps = draw_sweeps(jax.random.fold_in(key_of[6], 71), 0)
    targets = draw_targets(jax.random.fold_in(key_of[6], 71), 0)
    matrix_ids = touch_ends(jax.random.randint(key_of[3], (BLOCKS, PAIRS, 2), 0, MATS), jax.random.fold_in(key_of[3], 1), 0, MATS - 1).astype(jnp.int32)
    self_ids = touch_ends(jax.random.randint(key_of[4], (BLOCKS, 2), 0, MATS), jax.random.fold_in(key_of[4], 1), 0, MATS - 1).astype(jnp.int32)
    vertical = bell_draw(key_of[5], (2 * REACH + 1, LEVELS, BLOCKS), 0.25, 1.0, ((1, 8), (2, 32)), jnp.float32)
    return {"tracers": tracers, "sweeps": sweeps, "targets": targets, "matrix_ids": matrix_ids, "self_ids": self_ids, "vertical": vertical}


def sweep_pair(block_rows, sweeps, first_ids, second_ids):
    first_sweep = jnp.einsum("prc,pcd->prd", block_rows.astype(jnp.float32), sweeps[0][first_ids].astype(jnp.float32), precision=lax.Precision.HIGHEST).astype(jnp.bfloat16)
    return jnp.einsum("prc,pcd->prd", first_sweep.astype(jnp.float32), sweeps[1][second_ids].astype(jnp.float32), precision=lax.Precision.HIGHEST)


def reference(tracers, sweeps, targets, matrix_ids, self_ids, vertical):
    block_rows = tracers.reshape(BLOCKS, TRACERS * LEVELS, BS)

    def own_step(step_index):
        pair_start = step_index * BLOCKS_DEV
        part_rows = lax.dynamic_slice_in_dim(block_rows, pair_start, BLOCKS_DEV, 0)
        pair_ids = lax.dynamic_slice_in_dim(self_ids, pair_start, BLOCKS_DEV, 0)
        return sweep_pair(part_rows, sweeps, pair_ids[:, 0], pair_ids[:, 1])

    own_term = lax.map(own_step, jnp.arange(N_TILE, dtype=jnp.int32)).reshape(BLOCKS, TRACERS * LEVELS, BS)
    flat_targets = targets.reshape(-1)
    flat_ids = matrix_ids.reshape(-1, 2)

    def pair_step(running, step_index):
        pair_start = step_index * BLOCKS_DEV
        pair_index = pair_start + jnp.arange(BLOCKS_DEV, dtype=jnp.int32)
        source_rows = block_rows[pair_index // PAIRS]
        pair_ids = lax.dynamic_slice_in_dim(flat_ids, pair_start, BLOCKS_DEV, 0)
        partial_value = sweep_pair(source_rows, sweeps, pair_ids[:, 0], pair_ids[:, 1]).astype(jnp.bfloat16)
        arrival = lax.dynamic_slice_in_dim(flat_targets, pair_start, BLOCKS_DEV, 0)
        return running.at[arrival].add(partial_value.astype(jnp.float32)), None

    summed, _ = lax.scan(pair_step, own_term, jnp.arange(PAIRS * N_TILE, dtype=jnp.int32))
    arrived = summed.astype(jnp.bfloat16).reshape(BLOCKS, TRACERS, LEVELS, BS)
    padded = jnp.pad(arrived, ((0, 0), (0, 0), (REACH, REACH), (0, 0)))
    weights = jnp.transpose(vertical, (0, 2, 1))
    remapped = arrived.astype(jnp.float32)
    for offset in range(2 * REACH + 1):
        remapped = remapped + weights[offset][:, None, :, None] * padded[:, :, offset:offset + LEVELS, :].astype(jnp.float32)
    return remapped.astype(jnp.bfloat16)
```

```python
import functools

import jax
import jax.numpy as jnp
from jax import lax
from jax.experimental import pallas as pl
from jax.experimental.pallas import tpu as pltpu
from jax.sharding import PartitionSpec as P

MESH = pl.DeviceIdType.MESH
REACH = 4
XN, ZN = 4, 8
TILES = XN * ZN
BLOCKS = 256
CELLS = 128
TRACERS = 4
LEVS = 8
ROWS = TRACERS * LEVS
SHARE = 24
TAP = 2 * REACH + 1
HEAD = 16
PART = SHARE * LEVS
MSG = HEAD + TRACERS * PART
HALF = 384
PITCH = BLOCKS + 8
SLOTS = TILES * SHARE
f32, bf16, i32 = jnp.float32, jnp.bfloat16, jnp.int32


def dot(a, b):
    return jnp.dot(a, b, preferred_element_type=f32)


def plan_kernel(ids_ref, table_ref, index_ref):
    me = lax.axis_index("tile")
    lane = lax.broadcasted_iota(i32, (BLOCKS, 128), 1)
    sub = lax.broadcasted_iota(i32, (BLOCKS, 128), 0)
    before = (
        lax.broadcasted_iota(i32, (BLOCKS, BLOCKS), 1) < lax.broadcasted_iota(i32, (BLOCKS, BLOCKS), 0)
    ).astype(f32).astype(bf16)
    ids = ids_ref[...]
    base = jnp.zeros((1, 128), f32)
    here = None
    total = None
    for j in range(3):
        target = ids[:, j : j + 1]
        apart = ((target >> 8) - me) & (TILES - 1)
        hits = (jnp.broadcast_to(apart, (BLOCKS, 128)) == lane).astype(f32)
        earlier = dot(before, hits.astype(bf16)) + base
        rank = jnp.sum(hits * earlier, axis=1, keepdims=True).astype(i32)
        base = base + jnp.sum(hits, axis=0, keepdims=True)
        extra = rank >= SHARE
        row = jnp.where(extra, TILES, apart)
        entry = jnp.where(extra, rank - SHARE, rank)
        order = jnp.where(extra, me, apart) * SHARE + entry
        chosen = (jnp.broadcast_to(row, (BLOCKS, 128)) == lane).astype(f32)
        at_entry = (jnp.broadcast_to(entry, (BLOCKS, 128)) == lane).astype(f32)
        values = [
            at_entry * sub.astype(f32),
            at_entry * ids[:, 3 + 2 * j : 4 + 2 * j].astype(f32),
            at_entry * ids[:, 4 + 2 * j : 5 + 2 * j].astype(f32),
        ]
        arrival = ((target & (BLOCKS - 1)) + 1).astype(f32)
        for m in range(SLOTS // 128):
            at = (jnp.broadcast_to(order, (BLOCKS, 128)) == lane + 128 * m).astype(f32)
            values.append(at * arrival)
        part = dot(chosen.T.astype(bf16), jnp.concatenate(values, axis=1).astype(bf16))
        total = part if total is None else total + part
    total = total[:40]
    packed = total[:, :128] + 256.0 * total[:, 128:256] + 4096.0 * total[:, 256:384]
    table_ref[...] = packed.astype(i32)
    index_ref[...] = jnp.zeros_like(index_ref)
    for m in range(SLOTS // 128):
        index_ref[:, m, :] = total[:, 384 + 128 * m : 512 + 128 * m]
    index_ref[39] = jnp.broadcast_to((base[:, :1] > SHARE).astype(f32), (8, 128))


def main_kernel(
    table_ref, self_ref, tracers_ref, sweeps_ref, index_ref, vertical_ref, out_ref,
    stage, sbuf, rbuf, ebuf, own, chosen, pad, turned, weight, obuf,
    send_sem, recv_sem, ring_send, ring_recv, cross_send, cross_recv, halo_send, halo_recv, local_sem, out_sem,
):
    me = lax.axis_index("tile")
    lev = lax.axis_index("lev")
    x, z = me // ZN, me % ZN

    def tile_at(dx, dz):
        return ((x + dx + XN) % XN) * ZN + (z + dz + ZN) % ZN

    barrier = pltpu.get_barrier_semaphore()

    def greet(k, carry):
        pl.semaphore_signal(barrier, inc=1, device_id=((me + k) % TILES, lev), device_id_type=MESH)
        return carry

    lax.fori_loop(1, TILES, greet, 0)
    above, below = (lev + 1) % LEVS, (lev + LEVS - 1) % LEVS
    for other in (above, below):
        pl.semaphore_signal(barrier, inc=1, device_id=(me, other), device_id_type=MESH)

    def swept(block, first, second):
        half = dot(tracers_ref[block], sweeps_ref[first]).astype(bf16)
        return dot(half, sweeps_ref[16 + second])

    def build(k):
        for e in range(SHARE):
            v = table_ref[k, e]
            stage[pl.ds(e, ROWS, stride=SHARE), :] = swept(v & 255, (v >> 8) & 15, (v >> 12) & 15)
        sbuf[k, 0:HEAD] = jnp.concatenate([index_ref[k], jnp.zeros((8, 128), f32)], axis=0).astype(bf16)
        for t in range(TRACERS):
            sbuf[k, HEAD + t * PART : HEAD + (t + 1) * PART] = stage[t * PART : (t + 1) * PART, :].astype(bf16)

    def span(t):
        return pl.ds(0, HEAD + PART) if t == 0 else pl.ds(HEAD + t * PART, PART)

    def send(t, k):
        return pltpu.make_async_remote_copy(
            src_ref=sbuf.at[k, span(t)], dst_ref=rbuf.at[k, span(t)],
            send_sem=send_sem.at[t], recv_sem=recv_sem.at[t],
            device_id=((me + k) % TILES, lev), device_id_type=MESH,
        )

    def wait_bytes(buf, t, sem):
        ref = buf.at[pl.ds(1, TILES - 1), span(t)]
        pltpu.make_async_copy(ref, ref, sem).wait()

    def ring(j, way):
        item = x * ZN + (z - way * j + ZN) % ZN
        rows = pl.ds(0, MSG) if j < 3 else (pl.ds(0, HALF) if way > 0 else pl.ds(HALF, MSG - HALF))
        d = 0 if way > 0 else 1
        return pltpu.make_async_remote_copy(
            src_ref=sbuf.at[TILES, rows] if j == 0 else ebuf.at[item, rows],
            dst_ref=ebuf.at[item, rows],
            send_sem=ring_send.at[d, j], recv_sem=ring_recv.at[d, j],
            device_id=(tile_at(0, way), lev), device_id_type=MESH,
        )

    def cross(dx):
        group = pl.ds(x * ZN, ZN)
        return pltpu.make_async_remote_copy(
            src_ref=ebuf.at[group], dst_ref=ebuf.at[group],
            send_sem=cross_send.at[dx - 1], recv_sem=cross_recv.at[dx - 1],
            device_id=(tile_at(dx, 0), lev), device_id_type=MESH,
        )

    def keep(src, dst, i):
        return pltpu.make_async_copy(src, dst, local_sem.at[i])

    keep_extra = keep(sbuf.at[TILES], ebuf.at[me], 0)
    keep_main = keep(sbuf.at[0], rbuf.at[0], 1)
    stops = (7, 13, 19, 25)

    def step(i, carry):
        k = jnp.where(i == 0, TILES, jnp.where(i == TILES, 0, i))
        build(k)

        @pl.when(i == 0)
        def _():
            pl.semaphore_wait(barrier, TILES + 1)
            ring(0, 1).start()
            ring(0, -1).start()
            keep_extra.start()

        @pl.when(jnp.logical_and(i > 0, i < TILES))
        def _():
            send(0, k).start()

        for j, stop in enumerate(stops):
            @pl.when(i == stop)
            def _():
                for way in (1, -1):
                    ring(j, way).wait_recv()
                if j == 0:
                    keep_extra.wait()
                if j < 3:
                    for way in (1, -1):
                        ring(j + 1, way).start()
                else:
                    for dx in (1, 3, 2):
                        cross(dx).start()

        return carry

    lax.fori_loop(0, TILES + 1, step, 0)
    keep_main.start()

    def send_phase(t):
        def one(k, carry):
            send(t, k).start()
            return carry

        lax.fori_loop(1, TILES, one, 0)

    send_phase(1)

    def own_step(g, carry):
        for u in range(8):
            b = g * 8 + u
            v = self_ref[b]
            own[pl.ds(b, ROWS, stride=PITCH), :] = swept(b, v & 15, (v >> 4) & 15)
        return carry

    lax.fori_loop(0, BLOCKS // 8, own_step, 0)

    tap_row = lax.broadcasted_iota(i32, (TAP * LEVS, BLOCKS), 0)
    source = lev * LEVS + tap_row % LEVS + tap_row // LEVS - REACH
    plain = vertical_ref[...] + jnp.where(tap_row // LEVS == REACH, 1.0, 0.0)
    turned[:, : TAP * LEVS] = jnp.where(jnp.logical_and(source >= 0, source < LEVS * LEVS), plain, 0.0).T

    def spread(g, carry):
        rows = pl.ds(pl.multiple_of(g * 8, 8), 8)
        columns = turned[rows, :]
        for n in range(TAP * LEVS):
            weight[n, rows] = jnp.broadcast_to(columns[:, n : n + 1], (8, CELLS))
        return carry

    lax.fori_loop(0, BLOCKS // 8, spread, 0)

    def choose(buf, first, hot):
        def add(s, tile):
            return tile + buf[s, 0:HEAD].astype(f32)

        tile = lax.fori_loop(0, TILES, add, jnp.zeros((HEAD, 128), f32))
        block = lax.broadcasted_iota(i32, (BLOCKS, 128), 0).astype(f32) + 1.0
        for m in range(SLOTS // 128):
            row = tile[m : m + 1]
            if hot is not None:
                row = row * hot
            hit = (jnp.broadcast_to(row, (BLOCKS, 128)) == block).astype(f32)
            chosen[:, first + 128 * m : first + 128 * (m + 1)] = hit.astype(bf16)

    def gather_sum(t):
        def pair(q, carry):
            rows = pl.ds(pl.multiple_of(HEAD + t * PART + q * 2 * SHARE, 16), 2 * SHARE)
            pieces = [buf[s, rows].astype(f32) for buf in (rbuf, ebuf) for s in range(TILES)]
            even = jnp.concatenate([p[:SHARE] for p in pieces], axis=0).astype(bf16)
            odd = jnp.concatenate([p[SHARE:] for p in pieces], axis=0).astype(bf16)
            both = dot(chosen[...], jnp.concatenate([even, odd], axis=1))
            for h in range(2):
                r = t * LEVS + 2 * q + h
                mine = own[pl.ds(pl.multiple_of(r * PITCH, 8), BLOCKS), :]
                pad[t, REACH + 2 * q + h] = (mine + both[:, h * CELLS : (h + 1) * CELLS]).astype(bf16)
            return carry

        lax.fori_loop(0, LEVS // 2, pair, 0)

    def halo(t, way):
        inner = pl.ds(LEVS, REACH) if way > 0 else pl.ds(REACH, REACH)
        outer = pl.ds(0, REACH) if way > 0 else pl.ds(LEVS + REACH, REACH)
        d = 0 if way > 0 else 1
        return pltpu.make_async_remote_copy(
            src_ref=pad.at[t, inner], dst_ref=pad.at[t, outer],
            send_sem=halo_send.at[d, t], recv_sem=halo_recv.at[d, t],
            device_id=(me, above if way > 0 else below), device_id_type=MESH,
        )

    def write_out(t):
        span_out = pl.ds(t * LEVS, LEVS)
        return pltpu.make_async_copy(obuf.at[span_out], out_ref.at[span_out], out_sem.at[t])

    def remap(t):
        def chunk(g, carry):
            rows = pl.ds(pl.multiple_of(g * 16, 16), 16)
            levels = [pad[t, m, rows].astype(f32) for m in range(LEVS + 2 * REACH)]
            for l in range(LEVS):
                total = weight[l, rows] * levels[l]
                for n in range(1, TAP):
                    total = total + weight[n * LEVS + l, rows] * levels[l + n]
                obuf[t * LEVS + l, rows] = total.astype(bf16)
            return carry

        lax.fori_loop(0, BLOCKS // 16, chunk, 0)
        write_out(t).start()

    def finish(t):
        for way in (1, -1):
            halo(t, way).wait_recv()
        remap(t)

    keep_main.wait()
    for t in range(TRACERS):
        wait_bytes(sbuf, t, send_sem.at[t])
        if t + 2 < TRACERS:
            send_phase(t + 2)
        wait_bytes(rbuf, t, recv_sem.at[t])
        if t == 0:
            for dx in (1, 2, 3):
                cross(dx).wait_recv()
            choose(rbuf, 0, None)
            choose(ebuf, SLOTS, index_ref[39][0:1])
        gather_sum(t)
        for way in (1, -1):
            halo(t, way).start()
        if t > 0:
            finish(t - 1)
    finish(TRACERS - 1)
    for t in range(TRACERS):
        write_out(t).wait()
        for way in (1, -1):
            halo(t, way).wait_send()
    for j in range(4):
        for way in (1, -1):
            ring(j, way).wait_send()
    for dx in (1, 2, 3):
        cross(dx).wait_send()


def on_device(tracers, sweeps, targets, matrix_ids, self_ids, vertical):
    vmem = pl.BlockSpec(memory_space=pltpu.VMEM)
    smem = pl.BlockSpec(memory_space=pltpu.SMEM)
    ids = jnp.concatenate([targets, matrix_ids.reshape(BLOCKS, 6)], axis=1)
    table, index = pl.pallas_call(
        plan_kernel,
        name="plan",
        out_shape=(jax.ShapeDtypeStruct((40, 128), i32), jax.ShapeDtypeStruct((40, 8, 128), f32)),
        in_specs=[vmem],
        out_specs=(vmem, vmem),
    )(ids)
    own_ids = self_ids[:, 0] + 16 * self_ids[:, 1]
    dma = pltpu.SemaphoreType.DMA
    out = pl.pallas_call(
        main_kernel,
        name="remap",
        out_shape=jax.ShapeDtypeStruct((ROWS, BLOCKS, CELLS), bf16),
        in_specs=[smem, smem, vmem, vmem, vmem, vmem],
        out_specs=pl.BlockSpec(memory_space=pl.ANY),
        scratch_shapes=[
            pltpu.VMEM((SHARE * ROWS, CELLS), f32),
            pltpu.VMEM((TILES + 1, MSG, CELLS), bf16),
            pltpu.VMEM((TILES, MSG, CELLS), bf16),
            pltpu.VMEM((TILES, MSG, CELLS), bf16),
            pltpu.VMEM((ROWS * PITCH, CELLS), f32),
            pltpu.VMEM((BLOCKS, 2 * SLOTS), bf16),
            pltpu.VMEM((TRACERS, LEVS + 2 * REACH, BLOCKS, CELLS), bf16),
            pltpu.VMEM((BLOCKS, 128), f32),
            pltpu.VMEM((TAP * LEVS, BLOCKS, CELLS), f32),
            pltpu.VMEM((ROWS, BLOCKS, CELLS), bf16),
            dma((TRACERS,)), dma((TRACERS,)), dma((2, 4)), dma((2, 4)), dma((3,)), dma((3,)),
            dma((2, TRACERS)), dma((2, TRACERS)), dma((2,)), dma((TRACERS,)),
        ],
        compiler_params=pltpu.CompilerParams(
            collective_id=0, has_side_effects=True, vmem_limit_bytes=56 * 1024 * 1024
        ),
    )(
        table,
        own_ids,
        tracers.reshape(BLOCKS, ROWS, CELLS),
        sweeps.reshape(-1, CELLS, CELLS),
        index,
        vertical.reshape(TAP * LEVS, BLOCKS),
    )
    return jnp.transpose(out, (1, 0, 2)).reshape(BLOCKS, TRACERS, LEVS, CELLS)


def solution(mesh):
    placed = (
        P("tile", None, "lev", None),
        P(),
        P("tile", None),
        P("tile", None, None),
        P("tile", None),
        P(None, "lev", "tile"),
    )
    return jax.shard_map(
        on_device,
        mesh=mesh,
        in_specs=placed,
        out_specs=P("tile", None, "lev", None),
        check_vma=False,
    )
```

```python
import functools

import jax
import jax.numpy as jnp
from jax import lax
from jax.experimental import pallas as pl
from jax.experimental.pallas import tpu as pltpu
from jax.sharding import PartitionSpec as P

MESH = pl.DeviceIdType.MESH
REACH = 4
XN, ZN = 4, 8
TILES = XN * ZN
BLOCKS = 256
CELLS = 128
TRACERS = 4
LEVS = 8
ROWS = TRACERS * LEVS
SHARE = 24
TAP = 2 * REACH + 1
HEAD = 16
PART = SHARE * LEVS
MSG = HEAD + TRACERS * PART
HALF = 384
PITCH = BLOCKS + 8
SLOTS = TILES * SHARE
STOPS = (5, 10, 15, 20)
f32, bf16, i32 = jnp.float32, jnp.bfloat16, jnp.int32


def dot(a, b):
    return jnp.dot(a, b, preferred_element_type=f32)


def main_kernel(
    target_ref, matrix_ref, self_ref, tracers_in, sweeps_in, vertical_in, out_ref,
    tracers_ref, sweeps_ref, vertical_ref, table_made, table_ref, index_ref,
    stage, sbuf, rbuf, ebuf, own, chosen, pad, turned, weight, turn, obuf,
    in_sem, send_sem, recv_sem, ring_send, ring_recv, cross_send, cross_recv, halo_send, halo_recv, local_sem, out_sem,
):
    me = lax.axis_index("tile")
    lev = lax.axis_index("lev")
    x, z = me // ZN, me % ZN

    def tile_at(dx, dz):
        return ((x + dx + XN) % XN) * ZN + (z + dz + ZN) % ZN

    def tile_of(k):
        return tile_at(k // ZN, k % ZN)

    loads = [
        pltpu.make_async_copy(src, dst, in_sem.at[n])
        for n, (src, dst) in enumerate(
            ((sweeps_in, sweeps_ref), (tracers_in, tracers_ref), (vertical_in, vertical_ref))
        )
    ]
    for load in loads:
        load.start()
    barrier = pltpu.get_barrier_semaphore()

    def greet(k, carry):
        pl.semaphore_signal(barrier, inc=1, device_id=(tile_of(k), lev), device_id_type=MESH)
        return carry

    lax.fori_loop(1, TILES, greet, 0)
    above, below = (lev + 1) % LEVS, (lev + LEVS - 1) % LEVS
    for other in (above, below):
        pl.semaphore_signal(barrier, inc=1, device_id=(me, other), device_id_type=MESH)

    def plan():
        sub = lax.broadcasted_iota(i32, (40, BLOCKS), 0)
        slot = lax.broadcasted_iota(i32, (SLOTS, BLOCKS), 0)
        block = lax.broadcasted_iota(i32, (1, BLOCKS), 1).astype(f32)
        before = (
            lax.broadcasted_iota(i32, (BLOCKS, BLOCKS), 0) < lax.broadcasted_iota(i32, (BLOCKS, BLOCKS), 1)
        ).astype(f32).astype(bf16)
        base = jnp.zeros((40, 1), f32)
        total = None
        for j in range(3):
            target = target_ref[j : j + 1, :]
            owner = target >> 8
            apart = (((owner >> 3) - x) & (XN - 1)) * ZN + (((owner & (ZN - 1)) - z) & (ZN - 1))
            hits = (jnp.broadcast_to(apart, (40, BLOCKS)) == sub).astype(f32)
            earlier = dot(hits.astype(bf16), before) + base
            rank = jnp.sum(hits * earlier, axis=0, keepdims=True).astype(i32)
            base = base + jnp.sum(hits, axis=1, keepdims=True)
            extra = rank >= SHARE
            row = jnp.where(extra, TILES, apart)
            entry = jnp.where(extra, rank - SHARE, rank)
            order = jnp.where(extra, me, apart) * SHARE + entry
            taken = (jnp.broadcast_to(row, (40, BLOCKS)) == sub).astype(f32).astype(bf16)
            at_entry = (jnp.broadcast_to(entry, (32, BLOCKS)) == sub[:32]).astype(f32)
            arrival = ((target & (BLOCKS - 1)) + 1).astype(f32)
            ids = matrix_ref[j].astype(f32)
            at = (jnp.broadcast_to(order, (SLOTS, BLOCKS)) == slot).astype(f32)
            values = jnp.concatenate(
                [at_entry * block, at_entry * ids[0:1], at_entry * ids[1:2], at_entry, at * arrival], axis=0
            ).astype(bf16)
            part = lax.dot_general(taken, values, (((1,), (1,)), ((), ())), preferred_element_type=f32)
            total = part if total is None else total + part
        table_made[...] = total[:, :128].astype(i32)
        for m in range(SLOTS // 128):
            index_ref[:, m, :] = total[:, 128 * (m + 1) : 128 * (m + 2)]
        for m in range(SLOTS // 128, 8):
            index_ref[:, m, :] = jnp.zeros((40, 128), f32)
        index_ref[39] = jnp.broadcast_to((base[0:1] > SHARE).astype(f32), (8, 128))
        copy = pltpu.make_async_copy(table_made, table_ref, in_sem.at[3])
        copy.start()
        copy.wait()

    plan()
    for load in loads:
        load.wait()

    def swept(block, first, second):
        half = dot(tracers_ref[block], sweeps_ref[first]).astype(bf16)
        return dot(half, sweeps_ref[16 + second])

    def build(k):
        for e in range(SHARE):
            stage[pl.ds(e, ROWS, stride=SHARE), :] = swept(
                table_ref[k, e] & (BLOCKS - 1), table_ref[k, 32 + e] & 15, table_ref[k, 64 + e] & 15
            )
        sbuf[k, 0:HEAD] = jnp.concatenate([index_ref[k], jnp.zeros((8, 128), f32)], axis=0).astype(bf16)
        for t in range(TRACERS):
            sbuf[k, HEAD + t * PART : HEAD + (t + 1) * PART] = stage[t * PART : (t + 1) * PART, :].astype(bf16)

    def span(t):
        return pl.ds(0, HEAD + PART) if t == 0 else pl.ds(HEAD + t * PART, PART)

    def send(t, k):
        return pltpu.make_async_remote_copy(
            src_ref=sbuf.at[k, span(t)], dst_ref=rbuf.at[k, span(t)],
            send_sem=send_sem.at[t], recv_sem=recv_sem.at[t],
            device_id=(tile_of(k), lev), device_id_type=MESH,
        )

    def wait_bytes(buf, t, sem):
        ref = buf.at[pl.ds(1, TILES - 1), span(t)]
        pltpu.make_async_copy(ref, ref, sem).wait()

    def ring(j, way):
        item = x * ZN + (z - way * j + ZN) % ZN
        rows = pl.ds(0, MSG) if j < 3 else (pl.ds(0, HALF) if way > 0 else pl.ds(HALF, MSG - HALF))
        d = 0 if way > 0 else 1
        return pltpu.make_async_remote_copy(
            src_ref=sbuf.at[TILES, rows] if j == 0 else ebuf.at[item, rows],
            dst_ref=ebuf.at[item, rows],
            send_sem=ring_send.at[d, j], recv_sem=ring_recv.at[d, j],
            device_id=(tile_at(0, way), lev), device_id_type=MESH,
        )

    def cross(n):
        way = 1 if n % 2 == 0 else -1
        first = (x if n < 2 else (x - way + XN) % XN) * ZN
        group = pl.ds(first, ZN) if n < 2 else pl.ds(first if way > 0 else first + ZN // 2, ZN // 2)
        return pltpu.make_async_remote_copy(
            src_ref=ebuf.at[group], dst_ref=ebuf.at[group],
            send_sem=cross_send.at[n], recv_sem=cross_recv.at[n],
            device_id=(tile_at(way, 0), lev), device_id_type=MESH,
        )

    def keep(src, dst, i):
        return pltpu.make_async_copy(src, dst, local_sem.at[i])

    keep_extra = keep(sbuf.at[TILES], ebuf.at[me], 0)
    keep_main = keep(sbuf.at[0], rbuf.at[0], 1)
    stops = STOPS

    def step(i, carry):
        p = i - 1
        side = jnp.where(p % 2 == 0, p // 8 + 1, ZN - 1 - p // 8)
        dz = jnp.where(p < 24, side, jnp.where(p < 28, ZN // 2, 0))
        dx = jnp.where(p < 24, (p % 8) // 2, jnp.where(p < 28, p - 24, p - 27))
        k = jnp.where(i == 0, TILES, jnp.where(i == TILES, 0, dx * ZN + dz))
        build(k)

        @pl.when(i == 0)
        def _():
            pl.semaphore_wait(barrier, TILES + 1)
            ring(0, 1).start()
            ring(0, -1).start()
            keep_extra.start()

        @pl.when(jnp.logical_and(i > 0, i < TILES))
        def _():
            send(0, k).start()

        for j, stop in enumerate(stops):
            @pl.when(i == stop)
            def _():
                for way in (1, -1):
                    ring(j, way).wait_recv()
                if j < 3:
                    for way in (1, -1):
                        ring(j + 1, way).start()
                else:
                    keep_extra.wait()

        return carry

    lax.fori_loop(0, TILES + 1, step, 0)
    keep_main.start()

    def send_phase(t):
        def one(k, carry):
            send(t, k).start()
            return carry

        lax.fori_loop(1, TILES, one, 0)

    send_phase(1)
    cross(0).start()
    cross(1).start()

    def own_step(g, carry):
        for u in range(8):
            b = g * 8 + u
            own[pl.ds(b, ROWS, stride=PITCH), :] = swept(b, self_ref[0, b] & 15, self_ref[1, b] & 15)
        return carry

    lax.fori_loop(0, BLOCKS // 8, own_step, 0)
    wait_bytes(sbuf, 0, send_sem.at[0])
    send_phase(2)

    tap_row = lax.broadcasted_iota(i32, (TAP * LEVS, BLOCKS), 0)
    source = lev * LEVS + tap_row % LEVS + tap_row // LEVS - REACH
    plain = vertical_ref[...] + jnp.where(tap_row // LEVS == REACH, 1.0, 0.0)
    turned[:, : TAP * LEVS] = jnp.where(jnp.logical_and(source >= 0, source < LEVS * LEVS), plain, 0.0).T

    def spread(g, carry):
        rows = pl.ds(pl.multiple_of(g * 8, 8), 8)
        columns = turned[rows, :]
        for n in range(TAP * LEVS):
            weight[n, rows] = jnp.broadcast_to(columns[:, n : n + 1], (8, CELLS))
        return carry

    lax.fori_loop(0, BLOCKS // 8, spread, 0)
    for n in range(2):
        cross(n).wait_recv()
    for n in range(2, 4):
        cross(n).start()
    wait_bytes(sbuf, 1, send_sem.at[1])
    send_phase(3)

    def choose(buf, first, hot):
        def add(s, tile):
            return tile + buf[s, 0:HEAD].astype(f32)

        tile = lax.fori_loop(0, TILES, add, jnp.zeros((HEAD, 128), f32))
        block = lax.broadcasted_iota(i32, (BLOCKS, 128), 0).astype(f32) + 1.0
        for m in range(SLOTS // 128):
            row = tile[m : m + 1]
            if hot is not None:
                row = row * hot
            hit = (jnp.broadcast_to(row, (BLOCKS, 128)) == block).astype(f32)
            chosen[:, first + 128 * m : first + 128 * (m + 1)] = hit.astype(bf16)

    def halo(t, way):
        inner = pl.ds(LEVS, REACH) if way > 0 else pl.ds(REACH, REACH)
        outer = pl.ds(0, REACH) if way > 0 else pl.ds(LEVS + REACH, REACH)
        d = 0 if way > 0 else 1
        return pltpu.make_async_remote_copy(
            src_ref=pad.at[t, inner], dst_ref=pad.at[t, outer],
            send_sem=halo_send.at[d, t], recv_sem=halo_recv.at[d, t],
            device_id=(me, above if way > 0 else below), device_id_type=MESH,
        )

    def gather_sum(t):
        def pair(q, carry):
            rows = pl.ds(pl.multiple_of(HEAD + t * PART + q * 2 * SHARE, 16), 2 * SHARE)
            pieces = [buf[s, rows].astype(f32) for buf in (rbuf, ebuf) for s in range(TILES)]
            even = jnp.concatenate([p[:SHARE] for p in pieces], axis=0).astype(bf16)
            odd = jnp.concatenate([p[SHARE:] for p in pieces], axis=0).astype(bf16)
            both = dot(chosen[...], jnp.concatenate([even, odd], axis=1))
            for h in range(2):
                r = t * LEVS + 2 * q + h
                mine = own[pl.ds(pl.multiple_of(r * PITCH, 8), BLOCKS), :]
                pad[t, REACH + 2 * q + h] = (mine + both[:, h * CELLS : (h + 1) * CELLS]).astype(bf16)
            for n, way in ((1, -1), (3, 1)):
                @pl.when(q == n)
                def _():
                    halo(t, way).start()

            return carry

        lax.fori_loop(0, LEVS // 2, pair, 0)

    def write_out(t):
        return pltpu.make_async_copy(obuf.at[:, t], out_ref.at[:, t], out_sem.at[t])

    def remap(t):
        def chunk(g, carry):
            rows = pl.ds(pl.multiple_of(g * 16, 16), 16)
            levels = [pad[t, m, rows].astype(f32) for m in range(LEVS + 2 * REACH)]
            for l in range(LEVS):
                total = weight[l, rows] * levels[l]
                for n in range(1, TAP):
                    total = total + weight[n * LEVS + l, rows] * levels[l + n]
                turn[pl.ds(l, 16, stride=LEVS), :] = total
            for b in range(16):
                obuf[g * 16 + b, t] = turn[b * LEVS : (b + 1) * LEVS, :].astype(bf16)
            return carry

        lax.fori_loop(0, BLOCKS // 16, chunk, 0)
        write_out(t).start()

    def finish(t):
        for way in (1, -1):
            halo(t, way).wait_recv()
        remap(t)

    keep_main.wait()
    for t in range(TRACERS):
        wait_bytes(rbuf, t, recv_sem.at[t])
        if t == 0:
            for n in range(2, 4):
                cross(n).wait_recv()
            choose(rbuf, 0, None)
            choose(ebuf, SLOTS, index_ref[39][0:1])
        gather_sum(t)
        if t > 0:
            finish(t - 1)
    finish(TRACERS - 1)
    for t in range(TRACERS):
        write_out(t).wait()
        if t > 1:
            wait_bytes(sbuf, t, send_sem.at[t])
        for way in (1, -1):
            halo(t, way).wait_send()
    for n in range(4):
        for way in (1, -1):
            ring(n, way).wait_send()
        cross(n).wait_send()


def on_device(tracers, sweeps, targets, matrix_ids, self_ids, vertical):
    vmem = pl.BlockSpec(memory_space=pltpu.VMEM)
    smem = pl.BlockSpec(memory_space=pltpu.SMEM)
    hbm = pl.BlockSpec(memory_space=pl.ANY)
    dma = pltpu.SemaphoreType.DMA
    return pl.pallas_call(
        main_kernel,
        name="remap",
        out_shape=jax.ShapeDtypeStruct((BLOCKS, TRACERS, LEVS, CELLS), bf16),
        in_specs=[vmem, vmem, smem, hbm, hbm, hbm],
        out_specs=hbm,
        scratch_shapes=[
            pltpu.VMEM((BLOCKS, ROWS, CELLS), bf16),
            pltpu.VMEM((32, CELLS, CELLS), bf16),
            pltpu.VMEM((TAP * LEVS, BLOCKS), f32),
            pltpu.VMEM((40, 128), i32),
            pltpu.SMEM((40, 128), i32),
            pltpu.VMEM((40, 8, 128), f32),
            pltpu.VMEM((SHARE * ROWS, CELLS), f32),
            pltpu.VMEM((TILES + 1, MSG, CELLS), bf16),
            pltpu.VMEM((TILES, MSG, CELLS), bf16),
            pltpu.VMEM((TILES, MSG, CELLS), bf16),
            pltpu.VMEM((ROWS * PITCH, CELLS), f32),
            pltpu.VMEM((BLOCKS, 2 * SLOTS), bf16),
            pltpu.VMEM((TRACERS, LEVS + 2 * REACH, BLOCKS, CELLS), bf16),
            pltpu.VMEM((BLOCKS, 128), f32),
            pltpu.VMEM((TAP * LEVS, BLOCKS, CELLS), f32),
            pltpu.VMEM((16 * LEVS, CELLS), f32),
            pltpu.VMEM((BLOCKS, TRACERS, LEVS, CELLS), bf16),
            dma((4,)), dma((TRACERS,)), dma((TRACERS,)), dma((2, 4)), dma((2, 4)), dma((4,)), dma((4,)),
            dma((2, TRACERS)), dma((2, TRACERS)), dma((2,)), dma((TRACERS,)),
        ],
        compiler_params=pltpu.CompilerParams(
            collective_id=0, has_side_effects=True, vmem_limit_bytes=56 * 1024 * 1024
        ),
    )(
        targets.T,
        jnp.transpose(matrix_ids, (1, 2, 0)),
        self_ids.T,
        tracers.reshape(BLOCKS, ROWS, CELLS),
        sweeps.reshape(-1, CELLS, CELLS),
        vertical.reshape(TAP * LEVS, BLOCKS),
    )


def solution(mesh):
    placed = (
        P("tile", None, "lev", None),
        P(),
        P("tile", None),
        P("tile", None, None),
        P("tile", None),
        P(None, "lev", "tile"),
    )
    return jax.shard_map(
        on_device,
        mesh=mesh,
        in_specs=placed,
        out_specs=P("tile", None, "lev", None),
        check_vma=False,
    )
```

```python
import functools

import jax
import jax.numpy as jnp
from jax import lax
from jax.experimental import pallas as pl
from jax.experimental.pallas import tpu as pltpu
from jax.sharding import PartitionSpec as P

MESH = pl.DeviceIdType.MESH
REACH = 4
XN, ZN = 4, 8
TILES = XN * ZN
BLOCKS = 256
CELLS = 128
TRACERS = 4
LEVS = 8
ROWS = TRACERS * LEVS
SHARE = 24
TAP = 2 * REACH + 1
HEAD = 16
PART = SHARE * LEVS
MSG = HEAD + TRACERS * PART
HALF = 384
PITCH = BLOCKS + 8
SLOTS = TILES * SHARE
STOPS = (4, 8, 12, 16)
PHASES = TRACERS + 1
f32, bf16, i32 = jnp.float32, jnp.bfloat16, jnp.int32


def ORDER(i):
    return jnp.where(i % 2 == 0, TILES - 2 - i // 2, i // 2)


def dot(a, b):
    return jnp.dot(a, b, preferred_element_type=f32)


def main_kernel(
    target_ref, matrix_ref, self_ref, tracers_in, sweeps_in, vertical_in, out_ref,
    tracers_ref, sweeps_ref, vertical_ref, table_made, table_ref, head, hot,
    stage, sbuf, rbuf, ebuf, own, chosen, pad, turned, weight, turn, obuf,
    in_sem, send_sem, recv_sem, ring_send, ring_recv, cross_send, cross_recv, halo_send, halo_recv, local_sem, out_sem,
):
    me = lax.axis_index("tile")
    lev = lax.axis_index("lev")
    x, z = me // ZN, me % ZN

    def tile_at(dx, dz):
        return ((x + dx + XN) % XN) * ZN + (z + dz + ZN) % ZN

    def tile_of(k):
        return tile_at(k // ZN, k % ZN)

    loads = [
        pltpu.make_async_copy(src, dst, in_sem.at[n])
        for n, (src, dst) in enumerate(
            ((sweeps_in, sweeps_ref), (tracers_in, tracers_ref), (vertical_in, vertical_ref))
        )
    ]
    for load in loads:
        load.start()
    barrier = pltpu.get_barrier_semaphore()

    def greet(k, carry):
        pl.semaphore_signal(barrier, inc=1, device_id=(tile_of(k), lev), device_id_type=MESH)
        return carry

    lax.fori_loop(1, TILES, greet, 0)
    above, below = (lev + 1) % LEVS, (lev + LEVS - 1) % LEVS
    for other in (above, below):
        pl.semaphore_signal(barrier, inc=1, device_id=(me, other), device_id_type=MESH)

    def plan():
        def over_blocks(a, b):
            return lax.dot_general(a, b.astype(bf16), (((1,), (1,)), ((), ())), preferred_element_type=f32)

        sub = lax.broadcasted_iota(i32, (40, BLOCKS), 0)
        slot = lax.broadcasted_iota(i32, (SLOTS, BLOCKS), 0)
        block = lax.broadcasted_iota(i32, (1, BLOCKS), 1).astype(f32)
        before = (
            lax.broadcasted_iota(i32, (BLOCKS, BLOCKS), 0) < lax.broadcasted_iota(i32, (BLOCKS, BLOCKS), 1)
        ).astype(f32).astype(bf16)
        base = jnp.zeros((40, 1), f32)
        line = lax.broadcasted_iota(i32, (8, BLOCKS), 0)
        total, index = None, None
        for j in range(3):
            target = target_ref[j : j + 1, :]
            owner = target >> 8
            apart = (((owner >> 3) - x) & (XN - 1)) * ZN + (((owner & (ZN - 1)) - z) & (ZN - 1))
            hits = (jnp.broadcast_to(apart, (40, BLOCKS)) == sub).astype(f32)
            earlier = dot(hits.astype(bf16), before) + base
            rank = jnp.sum(hits * earlier, axis=0, keepdims=True).astype(i32)
            base = base + jnp.sum(hits, axis=1, keepdims=True)
            extra = rank >= SHARE
            row = jnp.where(extra, TILES, apart)
            entry = jnp.where(extra, rank - SHARE, rank)
            order = jnp.where(extra, me, apart) * SHARE + entry
            taken = (jnp.broadcast_to(row, (40, BLOCKS)) == sub).astype(f32).astype(bf16)
            at_entry = (jnp.broadcast_to(entry, (32, BLOCKS)) == sub[:32]).astype(f32)
            arrival = ((target & (BLOCKS - 1)) + 1).astype(f32)
            ids = matrix_ref[j].astype(f32)
            at = (jnp.broadcast_to(order, (SLOTS, BLOCKS)) == slot).astype(f32)
            values = jnp.concatenate([at_entry * block, at_entry * ids[0:1], at_entry * ids[1:2], at_entry], axis=0)
            part = over_blocks(taken, values)
            total = part if total is None else total + part
            kind = (jnp.broadcast_to(extra.astype(i32), (8, BLOCKS)) == line).astype(f32).astype(bf16)
            part = over_blocks(kind, at * arrival)
            index = part if index is None else index + part
        table_made[...] = total.astype(i32)
        head[...] = jnp.zeros((HEAD, 128), f32)
        for m in range(SLOTS // 128):
            head[m : m + 1] = index[0:1, 128 * m : 128 * (m + 1)]
            head[8 + m : 9 + m] = index[1:2, 128 * m : 128 * (m + 1)]
        sbuf[TILES, 0:HEAD] = head[...].astype(bf16)
        hot[...] = jnp.broadcast_to((base[0:1] > SHARE).astype(f32), (8, 128))
        copy = pltpu.make_async_copy(table_made, table_ref, in_sem.at[3])
        copy.start()
        copy.wait()

    plan()
    for load in loads:
        load.wait()

    def swept(block, first, second):
        half = dot(tracers_ref[block], sweeps_ref[first]).astype(bf16)
        return dot(half, sweeps_ref[16 + second])

    def build(k):
        for e in range(SHARE):
            stage[pl.ds(e, ROWS, stride=SHARE), :] = swept(
                table_ref[k, e] & (BLOCKS - 1), table_ref[k, 32 + e] & 15, table_ref[k, 64 + e] & 15
            )
        for t in range(TRACERS):
            sbuf[k, HEAD + t * PART : HEAD + (t + 1) * PART] = stage[t * PART : (t + 1) * PART, :].astype(bf16)

    first_half = lev % 2

    def half_of(s):
        return first_half if s == TRACERS - 1 else 1 - first_half

    def span(s):
        if s < TRACERS - 1 or PHASES == TRACERS:
            return pl.ds(HEAD + s * PART, PART)
        start = HEAD + (TRACERS - 1) * PART + half_of(s) * (PART // 2)
        return pl.ds(pl.multiple_of(start, 16), PART // 2)

    def send(t, k):
        return pltpu.make_async_remote_copy(
            src_ref=sbuf.at[k, span(t)], dst_ref=rbuf.at[k, span(t)],
            send_sem=send_sem.at[t], recv_sem=recv_sem.at[t],
            device_id=(tile_of(k), lev), device_id_type=MESH,
        )

    def wait_bytes(buf, t, sem):
        ref = buf.at[pl.ds(1, TILES - 1), span(t)]
        pltpu.make_async_copy(ref, ref, sem).wait()

    def ring(j, way):
        item = x * ZN + (z - way * j + ZN) % ZN
        rows = pl.ds(0, MSG) if j < 3 else (pl.ds(0, HALF) if way > 0 else pl.ds(HALF, MSG - HALF))
        d = 0 if way > 0 else 1
        return pltpu.make_async_remote_copy(
            src_ref=sbuf.at[TILES, rows] if j == 0 else ebuf.at[item, rows],
            dst_ref=ebuf.at[item, rows],
            send_sem=ring_send.at[d, j], recv_sem=ring_recv.at[d, j],
            device_id=(tile_at(0, way), lev), device_id_type=MESH,
        )

    def cross(n):
        way = 1 if n % 2 == 0 else -1
        first = (x if n < 2 else (x - way + XN) % XN) * ZN
        group = pl.ds(first, ZN) if n < 2 else pl.ds(first if way > 0 else first + ZN // 2, ZN // 2)
        return pltpu.make_async_remote_copy(
            src_ref=ebuf.at[group], dst_ref=ebuf.at[group],
            send_sem=cross_send.at[n], recv_sem=cross_recv.at[n],
            device_id=(tile_at(way, 0), lev), device_id_type=MESH,
        )

    def keep(src, dst, i):
        return pltpu.make_async_copy(src, dst, local_sem.at[i])

    keep_extra = keep(sbuf.at[TILES], ebuf.at[me], 0)
    keep_main = keep(sbuf.at[0], rbuf.at[0], 1)
    def partner(p):
        side = jnp.where(p % 2 == 0, p // 8 + 1, ZN - 1 - p // 8)
        dz = jnp.where(p < 24, side, jnp.where(p < 28, ZN // 2, 0))
        dx = jnp.where(p < 24, (p % 8) // 2, jnp.where(p < 28, p - 24, p - 27))
        return dx * ZN + dz

    stops = STOPS

    def step(i, carry):
        k = jnp.where(i == 0, TILES, jnp.where(i == TILES, 0, partner(i - 1)))
        build(k)

        @pl.when(i == 0)
        def _():
            pl.semaphore_wait(barrier, TILES + 1)
            ring(0, 1).start()
            ring(0, -1).start()
            keep_extra.start()

        @pl.when(jnp.logical_and(i > 0, i < TILES))
        def _():
            send(0, k).start()

        for j, stop in enumerate(stops):
            @pl.when(i == stop)
            def _():
                for way in (1, -1):
                    ring(j, way).wait_recv()
                if j < 3:
                    for way in (1, -1):
                        ring(j + 1, way).start()
                else:
                    keep_extra.wait()

        return carry

    lax.fori_loop(0, TILES + 1, step, 0)
    keep_main.start()

    def send_phase(t):
        def one(i, carry):
            send(t, partner(ORDER(i))).start()
            return carry

        lax.fori_loop(0, TILES - 1, one, 0)

    send_phase(1)
    cross(0).start()
    cross(1).start()

    def own_step(g, carry):
        for u in range(8):
            b = g * 8 + u
            own[pl.ds(b, ROWS, stride=PITCH), :] = swept(b, self_ref[0, b] & 15, self_ref[1, b] & 15)
        return carry

    lax.fori_loop(0, BLOCKS // 8, own_step, 0)
    wait_bytes(sbuf, 0, send_sem.at[0])
    send_phase(2)

    tap_row = lax.broadcasted_iota(i32, (TAP * LEVS, BLOCKS), 0)
    source = lev * LEVS + tap_row % LEVS + tap_row // LEVS - REACH
    plain = vertical_ref[...] + jnp.where(tap_row // LEVS == REACH, 1.0, 0.0)
    turned[:, : TAP * LEVS] = jnp.where(jnp.logical_and(source >= 0, source < LEVS * LEVS), plain, 0.0).T

    def spread(g, carry):
        rows = pl.ds(pl.multiple_of(g * 8, 8), 8)
        columns = turned[rows, :]
        for n in range(TAP * LEVS):
            weight[n, rows] = jnp.broadcast_to(columns[:, n : n + 1], (8, CELLS))
        return carry

    lax.fori_loop(0, BLOCKS // 8, spread, 0)
    for n in range(2):
        cross(n).wait_recv()
    for n in range(2, 4):
        cross(n).start()
    wait_bytes(sbuf, 1, send_sem.at[1])
    send_phase(3)
    send_phase(4)

    def choose():
        lane = lax.broadcasted_iota(i32, (8, 128), 0) * 128 + lax.broadcasted_iota(i32, (8, 128), 1)

        def add(s, sums):
            tile = ebuf[s, 0:HEAD].astype(f32)
            k = ((x - s // ZN + XN) % XN) * ZN + (z - s % ZN + ZN) % ZN
            mine = jnp.logical_and(lane >= k * SHARE, lane < (k + 1) * SHARE)
            return sums[0] + jnp.where(mine, tile[0:8], 0.0), sums[1] + tile[8:16]

        none = jnp.zeros((8, 128), f32)
        main, extra = lax.fori_loop(0, TILES, add, (none, none))
        extra = extra * hot[...]
        block = lax.broadcasted_iota(i32, (BLOCKS, 128), 0).astype(f32) + 1.0
        for first, tile in ((0, main), (SLOTS, extra)):
            for m in range(SLOTS // 128):
                hit = (jnp.broadcast_to(tile[m : m + 1], (BLOCKS, 128)) == block).astype(f32)
                chosen[:, first + 128 * m : first + 128 * (m + 1)] = hit.astype(bf16)

    def halo(t, half):
        return pltpu.make_async_remote_copy(
            src_ref=pad.at[t, pl.ds(REACH + REACH * half, REACH)],
            dst_ref=pad.at[t, pl.ds((LEVS + REACH) * (1 - half), REACH)],
            send_sem=halo_send.at[half, t], recv_sem=halo_recv.at[half, t],
            device_id=(me, (lev + LEVS - 1 + 2 * half) % LEVS), device_id_type=MESH,
        )

    def gather_sum(t, half):
        def pair(n, carry):
            q = half * 2 + n
            rows = pl.ds(pl.multiple_of(HEAD + t * PART + q * 2 * SHARE, 16), 2 * SHARE)
            pieces = [buf[s, rows].astype(f32) for buf in (rbuf, ebuf) for s in range(TILES)]
            even = jnp.concatenate([p[:SHARE] for p in pieces], axis=0).astype(bf16)
            odd = jnp.concatenate([p[SHARE:] for p in pieces], axis=0).astype(bf16)
            both = dot(chosen[...], jnp.concatenate([even, odd], axis=1))
            for h in range(2):
                r = t * LEVS + 2 * q + h
                mine = own[pl.ds(pl.multiple_of(r * PITCH, 8), BLOCKS), :]
                pad[t, REACH + 2 * q + h] = (mine + both[:, h * CELLS : (h + 1) * CELLS]).astype(bf16)
            return carry

        lax.fori_loop(0, 2, pair, 0)
        halo(t, half).start()

    def write_out(t, c):
        part = pl.ds(c * (BLOCKS // 4), BLOCKS // 4)
        return pltpu.make_async_copy(obuf.at[part, t], out_ref.at[part, t], out_sem.at[t, c])

    def remap(t):
        def chunk(g, carry):
            rows = pl.ds(pl.multiple_of(g * 16, 16), 16)
            levels = [pad[t, m, rows].astype(f32) for m in range(LEVS + 2 * REACH)]
            for l in range(LEVS):
                total = weight[l, rows] * levels[l]
                for n in range(1, TAP):
                    total = total + weight[n * LEVS + l, rows] * levels[l + n]
                turn[pl.ds(l, 16, stride=LEVS), :] = total
            for b in range(16):
                obuf[g * 16 + b, t] = turn[b * LEVS : (b + 1) * LEVS, :].astype(bf16)

            @pl.when(g % 4 == 3)
            def _():
                write_out(t, g // 4).start()

            return carry

        lax.fori_loop(0, BLOCKS // 16, chunk, 0)

    def finish(t):
        for half in range(2):
            halo(t, half).wait_recv()
        remap(t)

    keep_main.wait()
    for s in range(PHASES):
        wait_bytes(rbuf, s, recv_sem.at[s])
        if s == 0:
            for n in range(2, 4):
                cross(n).wait_recv()
            choose()
        if s < TRACERS - 1 or PHASES == TRACERS:
            gather_sum(s, first_half)
            gather_sum(s, 1 - first_half)
        else:
            gather_sum(TRACERS - 1, half_of(s))
        if 0 < s < TRACERS:
            finish(s - 1)
    finish(TRACERS - 1)
    for s in range(2, PHASES):
        wait_bytes(sbuf, s, send_sem.at[s])
    for t in range(TRACERS):
        for c in range(4):
            write_out(t, c).wait()
        for half in range(2):
            halo(t, half).wait_send()
    for n in range(4):
        for way in (1, -1):
            ring(n, way).wait_send()
        cross(n).wait_send()


def hand_on(given_ref, out_ref, held, in_sem, out_sem):
    parts = [pl.ds(n * (BLOCKS // 4), BLOCKS // 4) for n in range(4)]
    loads = [pltpu.make_async_copy(given_ref.at[p], held.at[p], in_sem.at[n]) for n, p in enumerate(parts)]
    stores = [pltpu.make_async_copy(held.at[p], out_ref.at[p], out_sem.at[n]) for n, p in enumerate(parts)]
    for load in loads:
        load.start()
    for load, store in zip(loads, stores):
        load.wait()
        store.start()
    for store in stores:
        store.wait()


def on_device(tracers, sweeps, targets, matrix_ids, self_ids, vertical):
    vmem = pl.BlockSpec(memory_space=pltpu.VMEM)
    smem = pl.BlockSpec(memory_space=pltpu.SMEM)
    hbm = pl.BlockSpec(memory_space=pl.ANY)
    dma = pltpu.SemaphoreType.DMA
    remapped = pl.pallas_call(
        main_kernel,
        name="remap",
        out_shape=jax.ShapeDtypeStruct((BLOCKS, TRACERS, LEVS, CELLS), bf16),
        in_specs=[vmem, vmem, smem, hbm, hbm, hbm],
        out_specs=hbm,
        scratch_shapes=[
            pltpu.VMEM((BLOCKS, ROWS, CELLS), bf16),
            pltpu.VMEM((32, CELLS, CELLS), bf16),
            pltpu.VMEM((TAP * LEVS, BLOCKS), f32),
            pltpu.VMEM((40, 128), i32),
            pltpu.SMEM((40, 128), i32),
            pltpu.VMEM((HEAD, 128), f32),
            pltpu.VMEM((8, 128), f32),
            pltpu.VMEM((SHARE * ROWS, CELLS), f32),
            pltpu.VMEM((TILES + 1, MSG, CELLS), bf16),
            pltpu.VMEM((TILES, MSG, CELLS), bf16),
            pltpu.VMEM((TILES, MSG, CELLS), bf16),
            pltpu.VMEM((ROWS * PITCH, CELLS), f32),
            pltpu.VMEM((BLOCKS, 2 * SLOTS), bf16),
            pltpu.VMEM((TRACERS, LEVS + 2 * REACH, BLOCKS, CELLS), bf16),
            pltpu.VMEM((BLOCKS, 128), f32),
            pltpu.VMEM((TAP * LEVS, BLOCKS, CELLS), f32),
            pltpu.VMEM((16 * LEVS, CELLS), f32),
            pltpu.VMEM((BLOCKS, TRACERS, LEVS, CELLS), bf16),
            dma((4,)), dma((PHASES,)), dma((PHASES,)), dma((2, 4)), dma((2, 4)), dma((4,)), dma((4,)),
            dma((2, TRACERS)), dma((2, TRACERS)), dma((2,)), dma((TRACERS, 4)),
        ],
        compiler_params=pltpu.CompilerParams(
            collective_id=0, has_side_effects=True, vmem_limit_bytes=56 * 1024 * 1024
        ),
    )(
        targets.T,
        jnp.transpose(matrix_ids, (1, 2, 0)),
        self_ids.T,
        tracers.reshape(BLOCKS, ROWS, CELLS),
        sweeps.reshape(-1, CELLS, CELLS),
        vertical.reshape(TAP * LEVS, BLOCKS),
    )
    return pl.pallas_call(
        hand_on,
        name="hand_on",
        out_shape=jax.ShapeDtypeStruct(remapped.shape, bf16),
        in_specs=[hbm],
        out_specs=hbm,
        scratch_shapes=[pltpu.VMEM(remapped.shape, bf16), dma((4,)), dma((4,))],
        compiler_params=pltpu.CompilerParams(vmem_limit_bytes=56 * 1024 * 1024),
    )(remapped)


def solution(mesh):
    placed = (
        P("tile", None, "lev", None),
        P(),
        P("tile", None),
        P("tile", None, None),
        P("tile", None),
        P(None, "lev", "tile"),
    )
    return jax.shard_map(
        on_device,
        mesh=mesh,
        in_specs=placed,
        out_specs=P("tile", None, "lev", None),
        check_vma=False,
    )
```

```python
import functools

import jax
import jax.numpy as jnp
from jax import lax
from jax.experimental import pallas as pl
from jax.experimental.pallas import tpu as pltpu
from jax.sharding import PartitionSpec as P

MESH = pl.DeviceIdType.MESH
REACH = 4
XN, ZN = 4, 8
TILES = XN * ZN
BLOCKS = 256
CELLS = 128
TRACERS = 4
LEVS = 8
ROWS = TRACERS * LEVS
SHARE = 24
TAP = 2 * REACH + 1
HEAD = 16
PART = SHARE * LEVS
MSG = HEAD + TRACERS * PART
HALF = 384
PITCH = BLOCKS + 8
SLOTS = TILES * SHARE
STOPS = (4, 8, 12, 16)
PHASES = TRACERS + 1
f32, bf16, i32 = jnp.float32, jnp.bfloat16, jnp.int32


def ORDER(i):
    return jnp.where(i % 2 == 0, TILES - 2 - i // 2, i // 2)


def dot(a, b):
    return jnp.dot(a, b, preferred_element_type=f32)


def main_kernel(
    target_ref, matrix_ref, self_ref, tracers_in, sweeps_in, vertical_in, out_ref,
    tracers_ref, sweeps_ref, vertical_ref, table_made, table_ref, head, hot,
    stage, sbuf, rbuf, ebuf, own, chosen, pad, turned, weight, turn,
    in_sem, send_sem, recv_sem, ring_send, ring_recv, cross_send, cross_recv, halo_send, halo_recv, local_sem,
):
    me = lax.axis_index("tile")
    lev = lax.axis_index("lev")
    x, z = me // ZN, me % ZN

    def wrap(v, n):
        return jnp.where(v >= n, v - n, v)

    def tile_at(dx, dz):
        return wrap(x + dx, XN) * ZN + wrap(z + dz, ZN)

    def tile_of(k):
        return tile_at(k // ZN, k % ZN)

    loads = [
        pltpu.make_async_copy(src, dst, in_sem.at[n])
        for n, (src, dst) in enumerate(
            ((sweeps_in, sweeps_ref), (tracers_in, tracers_ref), (vertical_in, vertical_ref))
        )
    ]
    for load in loads:
        load.start()
    barrier = pltpu.get_barrier_semaphore()

    for dx in range(XN):
        for dz in range(ZN):
            if dx or dz:
                pl.semaphore_signal(barrier, inc=1, device_id=(tile_at(dx, dz), lev), device_id_type=MESH)
    above, below = (lev + 1) % LEVS, (lev + LEVS - 1) % LEVS
    for other in (above, below):
        pl.semaphore_signal(barrier, inc=1, device_id=(me, other), device_id_type=MESH)

    def plan():
        def over_blocks(a, b):
            return lax.dot_general(a, b.astype(bf16), (((1,), (1,)), ((), ())), preferred_element_type=f32)

        sub = lax.broadcasted_iota(i32, (40, BLOCKS), 0)
        slot = lax.broadcasted_iota(i32, (SLOTS, BLOCKS), 0)
        block = lax.broadcasted_iota(i32, (1, BLOCKS), 1).astype(f32)
        before = (
            lax.broadcasted_iota(i32, (BLOCKS, BLOCKS), 0) < lax.broadcasted_iota(i32, (BLOCKS, BLOCKS), 1)
        ).astype(f32).astype(bf16)
        base = jnp.zeros((40, 1), f32)
        line = lax.broadcasted_iota(i32, (8, BLOCKS), 0)
        total, index = None, None
        for j in range(3):
            target = target_ref[j : j + 1, :]
            owner = target >> 8
            apart = (((owner >> 3) - x) & (XN - 1)) * ZN + (((owner & (ZN - 1)) - z) & (ZN - 1))
            hits = (jnp.broadcast_to(apart, (40, BLOCKS)) == sub).astype(f32)
            earlier = dot(hits.astype(bf16), before) + base
            rank = jnp.sum(hits * earlier, axis=0, keepdims=True).astype(i32)
            base = base + jnp.sum(hits, axis=1, keepdims=True)
            extra = rank >= SHARE
            row = jnp.where(extra, TILES, apart)
            entry = jnp.where(extra, rank - SHARE, rank)
            order = jnp.where(extra, me, apart) * SHARE + entry
            taken = (jnp.broadcast_to(row, (40, BLOCKS)) == sub).astype(f32).astype(bf16)
            at_entry = (jnp.broadcast_to(entry, (32, BLOCKS)) == sub[:32]).astype(f32)
            arrival = ((target & (BLOCKS - 1)) + 1).astype(f32)
            ids = matrix_ref[j].astype(f32)
            at = (jnp.broadcast_to(order, (SLOTS, BLOCKS)) == slot).astype(f32)
            values = jnp.concatenate([at_entry * block, at_entry * ids[0:1], at_entry * ids[1:2], at_entry], axis=0)
            part = over_blocks(taken, values)
            total = part if total is None else total + part
            kind = (jnp.broadcast_to(extra.astype(i32), (8, BLOCKS)) == line).astype(f32).astype(bf16)
            part = over_blocks(kind, at * arrival)
            index = part if index is None else index + part
        table_made[...] = total.astype(i32)
        head[...] = jnp.zeros((HEAD, 128), f32)
        for m in range(SLOTS // 128):
            head[m : m + 1] = index[0:1, 128 * m : 128 * (m + 1)]
            head[8 + m : 9 + m] = index[1:2, 128 * m : 128 * (m + 1)]
        sbuf[TILES, 0:HEAD] = head[...].astype(bf16)
        hot[...] = jnp.broadcast_to((base[0:1] > SHARE).astype(f32), (8, 128))
        copy = pltpu.make_async_copy(table_made, table_ref, in_sem.at[3])
        copy.start()
        copy.wait()

    plan()
    for load in loads:
        load.wait()

    def swept(block, first, second):
        half = dot(tracers_ref[block], sweeps_ref[first]).astype(bf16)
        return dot(half, sweeps_ref[16 + second])

    def build(k):
        for e in range(SHARE):
            stage[pl.ds(e, ROWS, stride=SHARE), :] = swept(
                table_ref[k, e] & (BLOCKS - 1), table_ref[k, 32 + e] & 15, table_ref[k, 64 + e] & 15
            )
        for t in range(TRACERS):
            sbuf[k, HEAD + t * PART : HEAD + (t + 1) * PART] = stage[t * PART : (t + 1) * PART, :].astype(bf16)

    first_half = lev % 2

    def half_of(s):
        return first_half if s == TRACERS - 1 else 1 - first_half

    def span(s):
        if s < TRACERS - 1 or PHASES == TRACERS:
            return pl.ds(HEAD + s * PART, PART)
        start = HEAD + (TRACERS - 1) * PART + half_of(s) * (PART // 2)
        return pl.ds(pl.multiple_of(start, 16), PART // 2)

    def send(t, k):
        return pltpu.make_async_remote_copy(
            src_ref=sbuf.at[k, span(t)], dst_ref=rbuf.at[k, span(t)],
            send_sem=send_sem.at[t], recv_sem=recv_sem.at[t],
            device_id=(tile_of(k), lev), device_id_type=MESH,
        )

    def wait_bytes(buf, t, sem):
        ref = buf.at[pl.ds(1, TILES - 1), span(t)]
        pltpu.make_async_copy(ref, ref, sem).wait()

    def ring(j, way):
        item = x * ZN + (z - way * j + ZN) % ZN
        rows = pl.ds(0, MSG) if j < 3 else (pl.ds(0, HALF) if way > 0 else pl.ds(HALF, MSG - HALF))
        d = 0 if way > 0 else 1
        return pltpu.make_async_remote_copy(
            src_ref=sbuf.at[TILES, rows] if j == 0 else ebuf.at[item, rows],
            dst_ref=ebuf.at[item, rows],
            send_sem=ring_send.at[d, j], recv_sem=ring_recv.at[d, j],
            device_id=(tile_at(0, way % ZN), lev), device_id_type=MESH,
        )

    def cross(n):
        way = 1 if n % 2 == 0 else -1
        first = (x if n < 2 else (x - way + XN) % XN) * ZN
        group = pl.ds(first, ZN) if n < 2 else pl.ds(first if way > 0 else first + ZN // 2, ZN // 2)
        return pltpu.make_async_remote_copy(
            src_ref=ebuf.at[group], dst_ref=ebuf.at[group],
            send_sem=cross_send.at[n], recv_sem=cross_recv.at[n],
            device_id=(tile_at(way % XN, 0), lev), device_id_type=MESH,
        )

    def keep(src, dst, i):
        return pltpu.make_async_copy(src, dst, local_sem.at[i])

    keep_extra = keep(sbuf.at[TILES], ebuf.at[me], 0)
    keep_main = keep(sbuf.at[0], rbuf.at[0], 1)
    def partner(p):
        side = jnp.where(p % 2 == 0, p // 8 + 1, ZN - 1 - p // 8)
        dz = jnp.where(p < 24, side, jnp.where(p < 28, ZN // 2, 0))
        dx = jnp.where(p < 24, (p % 8) // 2, jnp.where(p < 28, p - 24, p - 27))
        return dx * ZN + dz

    stops = STOPS

    def step(i, carry):
        k = jnp.where(i == 0, TILES, jnp.where(i == TILES, 0, partner(i - 1)))
        build(k)

        @pl.when(i == 0)
        def _():
            pl.semaphore_wait(barrier, TILES + 1)
            ring(0, 1).start()
            ring(0, -1).start()
            keep_extra.start()

        @pl.when(jnp.logical_and(i > 0, i < TILES))
        def _():
            send(0, k).start()

        for j, stop in enumerate(stops):
            @pl.when(i == stop)
            def _():
                for way in (1, -1):
                    ring(j, way).wait_recv()
                if j < 3:
                    for way in (1, -1):
                        ring(j + 1, way).start()
                else:
                    keep_extra.wait()

        return carry

    lax.fori_loop(0, TILES + 1, step, 0)
    keep_main.start()

    def send_phase(t):
        def one(i, carry):
            send(t, partner(ORDER(i))).start()
            return carry

        lax.fori_loop(0, TILES - 1, one, 0)

    send_phase(1)
    cross(0).start()
    cross(1).start()

    def own_step(g, carry):
        for u in range(8):
            b = g * 8 + u
            own[pl.ds(b, ROWS, stride=PITCH), :] = swept(b, self_ref[0, b] & 15, self_ref[1, b] & 15)
        return carry

    lax.fori_loop(0, BLOCKS // 8, own_step, 0)
    wait_bytes(sbuf, 0, send_sem.at[0])
    send_phase(2)

    tap_row = lax.broadcasted_iota(i32, (TAP * LEVS, BLOCKS), 0)
    source = lev * LEVS + tap_row % LEVS + tap_row // LEVS - REACH
    plain = vertical_ref[...] + jnp.where(tap_row // LEVS == REACH, 1.0, 0.0)
    turned[:, : TAP * LEVS] = jnp.where(jnp.logical_and(source >= 0, source < LEVS * LEVS), plain, 0.0).T

    def spread(g, carry):
        rows = pl.ds(pl.multiple_of(g * 8, 8), 8)
        columns = turned[rows, :]
        for n in range(TAP * LEVS):
            weight[n, rows] = jnp.broadcast_to(columns[:, n : n + 1], (8, CELLS))
        return carry

    lax.fori_loop(0, BLOCKS // 8, spread, 0)
    for n in range(2):
        cross(n).wait_recv()
    for n in range(2, 4):
        cross(n).start()
    wait_bytes(sbuf, 1, send_sem.at[1])
    send_phase(3)
    send_phase(4)

    def choose():
        lane = lax.broadcasted_iota(i32, (8, 128), 0) * 128 + lax.broadcasted_iota(i32, (8, 128), 1)

        def add(s, sums):
            tile = ebuf[s, 0:HEAD].astype(f32)
            k = ((x - s // ZN + XN) % XN) * ZN + (z - s % ZN + ZN) % ZN
            mine = jnp.logical_and(lane >= k * SHARE, lane < (k + 1) * SHARE)
            return sums[0] + jnp.where(mine, tile[0:8], 0.0), sums[1] + tile[8:16]

        none = jnp.zeros((8, 128), f32)
        main, extra = lax.fori_loop(0, TILES, add, (none, none))
        extra = extra * hot[...]
        block = lax.broadcasted_iota(i32, (BLOCKS, 128), 0).astype(f32) + 1.0
        for first, tile in ((0, main), (SLOTS, extra)):
            for m in range(SLOTS // 128):
                hit = (jnp.broadcast_to(tile[m : m + 1], (BLOCKS, 128)) == block).astype(f32)
                chosen[:, first + 128 * m : first + 128 * (m + 1)] = hit.astype(bf16)

    def halo(t, half):
        return pltpu.make_async_remote_copy(
            src_ref=pad.at[t, pl.ds(REACH + REACH * half, REACH)],
            dst_ref=pad.at[t, pl.ds((LEVS + REACH) * (1 - half), REACH)],
            send_sem=halo_send.at[half, t], recv_sem=halo_recv.at[half, t],
            device_id=(me, (lev + LEVS - 1 + 2 * half) % LEVS), device_id_type=MESH,
        )

    def gather_sum(t, half):
        def pair(n, carry):
            q = half * 2 + n
            rows = pl.ds(pl.multiple_of(HEAD + t * PART + q * 2 * SHARE, 16), 2 * SHARE)
            pieces = [buf[s, rows].astype(f32) for buf in (rbuf, ebuf) for s in range(TILES)]
            even = jnp.concatenate([p[:SHARE] for p in pieces], axis=0).astype(bf16)
            odd = jnp.concatenate([p[SHARE:] for p in pieces], axis=0).astype(bf16)
            both = dot(chosen[...], jnp.concatenate([even, odd], axis=1))
            for h in range(2):
                r = t * LEVS + 2 * q + h
                mine = own[pl.ds(pl.multiple_of(r * PITCH, 8), BLOCKS), :]
                pad[t, REACH + 2 * q + h] = (mine + both[:, h * CELLS : (h + 1) * CELLS]).astype(bf16)
            return carry

        lax.fori_loop(0, 2, pair, 0)
        halo(t, half).start()

    def remap(t):
        def chunk(g, carry):
            rows = pl.ds(pl.multiple_of(g * 16, 16), 16)
            levels = [pad[t, m, rows].astype(f32) for m in range(LEVS + 2 * REACH)]
            for l in range(LEVS):
                total = weight[l, rows] * levels[l]
                for n in range(1, TAP):
                    total = total + weight[n * LEVS + l, rows] * levels[l + n]
                turn[pl.ds(l, 16, stride=LEVS), :] = total
            for b in range(16):
                out_ref[g * 16 + b, t] = turn[b * LEVS : (b + 1) * LEVS, :].astype(bf16)
            return carry

        lax.fori_loop(0, BLOCKS // 16, chunk, 0)

    def finish(t):
        for half in range(2):
            halo(t, half).wait_recv()
        remap(t)

    keep_main.wait()
    for s in range(PHASES):
        wait_bytes(rbuf, s, recv_sem.at[s])
        if s == 0:
            for n in range(2, 4):
                cross(n).wait_recv()
            choose()
        if s < TRACERS - 1 or PHASES == TRACERS:
            gather_sum(s, first_half)
            gather_sum(s, 1 - first_half)
        else:
            gather_sum(TRACERS - 1, half_of(s))
        if 0 < s < TRACERS:
            finish(s - 1)
    finish(TRACERS - 1)
    for s in range(2, PHASES):
        wait_bytes(sbuf, s, send_sem.at[s])
    for t in range(TRACERS):
        for half in range(2):
            halo(t, half).wait_send()
    for n in range(4):
        for way in (1, -1):
            ring(n, way).wait_send()
        cross(n).wait_send()


def on_device(tracers, sweeps, targets, matrix_ids, self_ids, vertical):
    vmem = pl.BlockSpec(memory_space=pltpu.VMEM)
    smem = pl.BlockSpec(memory_space=pltpu.SMEM)
    hbm = pl.BlockSpec(memory_space=pl.ANY)
    dma = pltpu.SemaphoreType.DMA
    return pl.pallas_call(
        main_kernel,
        name="remap",
        out_shape=pltpu.VMEM((BLOCKS, TRACERS, LEVS, CELLS), bf16),
        in_specs=[vmem, vmem, smem, hbm, hbm, hbm],
        out_specs=vmem,
        scratch_shapes=[
            pltpu.VMEM((BLOCKS, ROWS, CELLS), bf16),
            pltpu.VMEM((32, CELLS, CELLS), bf16),
            pltpu.VMEM((TAP * LEVS, BLOCKS), f32),
            pltpu.VMEM((40, 128), i32),
            pltpu.SMEM((40, 128), i32),
            pltpu.VMEM((HEAD, 128), f32),
            pltpu.VMEM((8, 128), f32),
            pltpu.VMEM((SHARE * ROWS, CELLS), f32),
            pltpu.VMEM((TILES + 1, MSG, CELLS), bf16),
            pltpu.VMEM((TILES, MSG, CELLS), bf16),
            pltpu.VMEM((TILES, MSG, CELLS), bf16),
            pltpu.VMEM((ROWS * PITCH, CELLS), f32),
            pltpu.VMEM((BLOCKS, 2 * SLOTS), bf16),
            pltpu.VMEM((TRACERS, LEVS + 2 * REACH, BLOCKS, CELLS), bf16),
            pltpu.VMEM((BLOCKS, 128), f32),
            pltpu.VMEM((TAP * LEVS, BLOCKS, CELLS), f32),
            pltpu.VMEM((16 * LEVS, CELLS), f32),
            dma((4,)), dma((PHASES,)), dma((PHASES,)), dma((2, 4)), dma((2, 4)), dma((4,)), dma((4,)),
            dma((2, TRACERS)), dma((2, TRACERS)), dma((2,)),
        ],
        compiler_params=pltpu.CompilerParams(
            collective_id=0, has_side_effects=True, vmem_limit_bytes=56 * 1024 * 1024
        ),
    )(
        targets.T,
        jnp.transpose(matrix_ids, (1, 2, 0)),
        self_ids.T,
        tracers.reshape(BLOCKS, ROWS, CELLS),
        sweeps.reshape(-1, CELLS, CELLS),
        vertical.reshape(TAP * LEVS, BLOCKS),
    )


def solution(mesh):
    placed = (
        P("tile", None, "lev", None),
        P(),
        P("tile", None),
        P("tile", None, None),
        P("tile", None),
        P(None, "lev", "tile"),
    )
    return jax.shard_map(
        on_device,
        mesh=mesh,
        in_specs=placed,
        out_specs=P("tile", None, "lev", None),
        check_vma=False,
    )
```

```python
import functools

import jax
import jax.numpy as jnp
from jax import lax
from jax.experimental import pallas as pl
from jax.experimental.pallas import tpu as pltpu
from jax.sharding import PartitionSpec as P

MESH = pl.DeviceIdType.MESH
REACH = 4
XN, ZN = 4, 8
TILES = XN * ZN
BLOCKS = 256
CELLS = 128
TRACERS = 4
LEVS = 8
ROWS = TRACERS * LEVS
SHARE = 24
TAP = 2 * REACH + 1
HEAD = 16
PART = SHARE * LEVS
MSG = HEAD + TRACERS * PART
HALF = 384
PITCH = BLOCKS + 8
SLOTS = TILES * SHARE
STOPS = (4, 8, 12, 16)
PHASES = TRACERS + 1
f32, bf16, i32 = jnp.float32, jnp.bfloat16, jnp.int32


def ORDER(i):
    return jnp.where(i % 2 == 0, TILES - 2 - i // 2, i // 2)


def dot(a, b):
    return jnp.dot(a, b, preferred_element_type=f32)


def main_kernel(
    target_in, matrix_in, self_in, tracers_in, sweeps_in, vertical_in, out_ref,
    target_ref, matrix_ref, self_ref,
    tracers_ref, sweeps_ref, vertical_ref, table_made, table_ref, head, hot,
    stage, sbuf, rbuf, ebuf, own, chosen, pad, turned, weight, turn,
    in_sem, send_sem, recv_sem, ring_send, ring_recv, cross_send, cross_recv, halo_send, halo_recv, local_sem,
):
    me = lax.axis_index("tile")
    lev = lax.axis_index("lev")
    x, z = me // ZN, me % ZN

    def wrap(v, n):
        return jnp.where(v >= n, v - n, v)

    def tile_at(dx, dz):
        return wrap(x + dx, XN) * ZN + wrap(z + dz, ZN)

    def tile_of(k):
        return tile_at(k // ZN, k % ZN)

    moves = (
        (target_in, target_ref), (matrix_in, matrix_ref), (self_in, self_ref),
        (sweeps_in, sweeps_ref), (tracers_in, tracers_ref), (vertical_in, vertical_ref),
    )
    loads = [pltpu.make_async_copy(src, dst, in_sem.at[n]) for n, (src, dst) in enumerate(moves)]
    for load in loads:
        load.start()
    barrier = pltpu.get_barrier_semaphore()

    for dx in range(XN):
        for dz in range(ZN):
            if dx or dz:
                pl.semaphore_signal(barrier, inc=1, device_id=(tile_at(dx, dz), lev), device_id_type=MESH)
    above, below = (lev + 1) % LEVS, (lev + LEVS - 1) % LEVS
    for other in (above, below):
        pl.semaphore_signal(barrier, inc=1, device_id=(me, other), device_id_type=MESH)

    def plan():
        def over_blocks(a, b):
            return lax.dot_general(a, b.astype(bf16), (((1,), (1,)), ((), ())), preferred_element_type=f32)

        sub = lax.broadcasted_iota(i32, (40, BLOCKS), 0)
        slot = lax.broadcasted_iota(i32, (SLOTS, BLOCKS), 0)
        block = lax.broadcasted_iota(i32, (1, BLOCKS), 1).astype(f32)
        before = (
            lax.broadcasted_iota(i32, (BLOCKS, BLOCKS), 0) < lax.broadcasted_iota(i32, (BLOCKS, BLOCKS), 1)
        ).astype(f32).astype(bf16)
        base = jnp.zeros((40, 1), f32)
        line = lax.broadcasted_iota(i32, (8, BLOCKS), 0)
        total, index = None, None
        for j in range(3):
            target = target_ref[j : j + 1, :]
            owner = target >> 8
            apart = (((owner >> 3) - x) & (XN - 1)) * ZN + (((owner & (ZN - 1)) - z) & (ZN - 1))
            hits = (jnp.broadcast_to(apart, (40, BLOCKS)) == sub).astype(f32)
            earlier = dot(hits.astype(bf16), before) + base
            rank = jnp.sum(hits * earlier, axis=0, keepdims=True).astype(i32)
            base = base + jnp.sum(hits, axis=1, keepdims=True)
            extra = rank >= SHARE
            row = jnp.where(extra, TILES, apart)
            entry = jnp.where(extra, rank - SHARE, rank)
            order = jnp.where(extra, me, apart) * SHARE + entry
            taken = (jnp.broadcast_to(row, (40, BLOCKS)) == sub).astype(f32).astype(bf16)
            at_entry = (jnp.broadcast_to(entry, (32, BLOCKS)) == sub[:32]).astype(f32)
            arrival = ((target & (BLOCKS - 1)) + 1).astype(f32)
            ids = matrix_ref[j].astype(f32)
            at = (jnp.broadcast_to(order, (SLOTS, BLOCKS)) == slot).astype(f32)
            values = jnp.concatenate([at_entry * block, at_entry * ids[0:1], at_entry * ids[1:2], at_entry], axis=0)
            part = over_blocks(taken, values)
            total = part if total is None else total + part
            kind = (jnp.broadcast_to(extra.astype(i32), (8, BLOCKS)) == line).astype(f32).astype(bf16)
            part = over_blocks(kind, at * arrival)
            index = part if index is None else index + part
        table_made[...] = total.astype(i32)
        head[...] = jnp.zeros((HEAD, 128), f32)
        for m in range(SLOTS // 128):
            head[m : m + 1] = index[0:1, 128 * m : 128 * (m + 1)]
            head[8 + m : 9 + m] = index[1:2, 128 * m : 128 * (m + 1)]
        sbuf[TILES, 0:HEAD] = head[...].astype(bf16)
        hot[...] = jnp.broadcast_to((base[0:1] > SHARE).astype(f32), (8, 128))
        copy = pltpu.make_async_copy(table_made, table_ref, in_sem.at[6])
        copy.start()
        copy.wait()

    for load in loads[:3]:
        load.wait()
    plan()
    for load in loads[3:]:
        load.wait()

    def swept(block, first, second):
        half = dot(tracers_ref[block], sweeps_ref[first]).astype(bf16)
        return dot(half, sweeps_ref[16 + second])

    def build(k):
        for e in range(SHARE):
            stage[pl.ds(e, ROWS, stride=SHARE), :] = swept(
                table_ref[k, e] & (BLOCKS - 1), table_ref[k, 32 + e] & 15, table_ref[k, 64 + e] & 15
            )
        for t in range(TRACERS):
            sbuf[k, HEAD + t * PART : HEAD + (t + 1) * PART] = stage[t * PART : (t + 1) * PART, :].astype(bf16)

    first_half = lev % 2

    def half_of(s):
        return first_half if s == TRACERS - 1 else 1 - first_half

    def span(s):
        if s < TRACERS - 1 or PHASES == TRACERS:
            return pl.ds(HEAD + s * PART, PART)
        start = HEAD + (TRACERS - 1) * PART + half_of(s) * (PART // 2)
        return pl.ds(pl.multiple_of(start, 16), PART // 2)

    def send(t, k):
        return pltpu.make_async_remote_copy(
            src_ref=sbuf.at[k, span(t)], dst_ref=rbuf.at[k, span(t)],
            send_sem=send_sem.at[t], recv_sem=recv_sem.at[t],
            device_id=(tile_of(k), lev), device_id_type=MESH,
        )

    def wait_bytes(buf, t, sem):
        ref = buf.at[pl.ds(1, TILES - 1), span(t)]
        pltpu.make_async_copy(ref, ref, sem).wait()

    def ring(j, way):
        item = x * ZN + (z - way * j + ZN) % ZN
        rows = pl.ds(0, MSG) if j < 3 else (pl.ds(0, HALF) if way > 0 else pl.ds(HALF, MSG - HALF))
        d = 0 if way > 0 else 1
        return pltpu.make_async_remote_copy(
            src_ref=sbuf.at[TILES, rows] if j == 0 else ebuf.at[item, rows],
            dst_ref=ebuf.at[item, rows],
            send_sem=ring_send.at[d, j], recv_sem=ring_recv.at[d, j],
            device_id=(tile_at(0, way % ZN), lev), device_id_type=MESH,
        )

    def cross(n):
        way = 1 if n % 2 == 0 else -1
        first = (x if n < 2 else (x - way + XN) % XN) * ZN
        group = pl.ds(first, ZN) if n < 2 else pl.ds(first if way > 0 else first + ZN // 2, ZN // 2)
        return pltpu.make_async_remote_copy(
            src_ref=ebuf.at[group], dst_ref=ebuf.at[group],
            send_sem=cross_send.at[n], recv_sem=cross_recv.at[n],
            device_id=(tile_at(way % XN, 0), lev), device_id_type=MESH,
        )

    def keep(src, dst, i):
        return pltpu.make_async_copy(src, dst, local_sem.at[i])

    keep_extra = keep(sbuf.at[TILES], ebuf.at[me], 0)
    keep_main = keep(sbuf.at[0], rbuf.at[0], 1)
    def partner(p):
        side = jnp.where(p % 2 == 0, p // 8 + 1, ZN - 1 - p // 8)
        side = jnp.where(lev % 2 == 0, side, ZN - side)
        dz = jnp.where(p < 24, side, jnp.where(p < 28, ZN // 2, 0))
        dx = jnp.where(p < 24, (p % 8) // 2, jnp.where(p < 28, p - 24, p - 27))
        return dx * ZN + dz

    stops = STOPS

    def step(i, carry):
        k = jnp.where(i == 0, TILES, jnp.where(i == TILES, 0, partner(i - 1)))
        build(k)

        @pl.when(i == 0)
        def _():
            pl.semaphore_wait(barrier, TILES + 1)
            ring(0, 1).start()
            ring(0, -1).start()
            keep_extra.start()

        @pl.when(jnp.logical_and(i > 0, i < TILES))
        def _():
            send(0, k).start()

        for j, stop in enumerate(stops):
            @pl.when(i == stop)
            def _():
                for way in (1, -1):
                    ring(j, way).wait_recv()
                if j < 3:
                    for way in (1, -1):
                        ring(j + 1, way).start()
                else:
                    keep_extra.wait()

        return carry

    lax.fori_loop(0, TILES + 1, step, 0)
    keep_main.start()

    def send_phase(t):
        def one(i, carry):
            send(t, partner(ORDER(i))).start()
            return carry

        lax.fori_loop(0, TILES - 1, one, 0)

    send_phase(1)
    cross(0).start()
    cross(1).start()

    def own_step(g, carry):
        for u in range(8):
            b = g * 8 + u
            own[pl.ds(b, ROWS, stride=PITCH), :] = swept(b, self_ref[0, b] & 15, self_ref[1, b] & 15)
        return carry

    lax.fori_loop(0, BLOCKS // 8, own_step, 0)
    wait_bytes(sbuf, 0, send_sem.at[0])
    send_phase(2)

    tap_row = lax.broadcasted_iota(i32, (TAP * LEVS, BLOCKS), 0)
    source = lev * LEVS + tap_row % LEVS + tap_row // LEVS - REACH
    plain = vertical_ref[...] + jnp.where(tap_row // LEVS == REACH, 1.0, 0.0)
    turned[:, : TAP * LEVS] = jnp.where(jnp.logical_and(source >= 0, source < LEVS * LEVS), plain, 0.0).T

    def spread(g, carry):
        rows = pl.ds(pl.multiple_of(g * 8, 8), 8)
        columns = turned[rows, :]
        for n in range(TAP * LEVS):
            weight[n, rows] = jnp.broadcast_to(columns[:, n : n + 1], (8, CELLS))
        return carry

    lax.fori_loop(0, BLOCKS // 8, spread, 0)
    for n in range(2):
        cross(n).wait_recv()
    for n in range(2, 4):
        cross(n).start()
    wait_bytes(sbuf, 1, send_sem.at[1])
    send_phase(3)
    send_phase(4)

    def choose():
        lane = lax.broadcasted_iota(i32, (8, 128), 0) * 128 + lax.broadcasted_iota(i32, (8, 128), 1)

        def add(s, sums):
            tile = ebuf[s, 0:HEAD].astype(f32)
            k = ((x - s // ZN + XN) % XN) * ZN + (z - s % ZN + ZN) % ZN
            mine = jnp.logical_and(lane >= k * SHARE, lane < (k + 1) * SHARE)
            return sums[0] + jnp.where(mine, tile[0:8], 0.0), sums[1] + tile[8:16]

        none = jnp.zeros((8, 128), f32)
        main, extra = lax.fori_loop(0, TILES, add, (none, none))
        extra = extra * hot[...]
        block = lax.broadcasted_iota(i32, (BLOCKS, 128), 0).astype(f32) + 1.0
        for first, tile in ((0, main), (SLOTS, extra)):
            for m in range(SLOTS // 128):
                hit = (jnp.broadcast_to(tile[m : m + 1], (BLOCKS, 128)) == block).astype(f32)
                chosen[:, first + 128 * m : first + 128 * (m + 1)] = hit.astype(bf16)

    def halo(t, q):
        half = q // 2
        return pltpu.make_async_remote_copy(
            src_ref=pad.at[t, pl.ds(REACH + 2 * q, 2)],
            dst_ref=pad.at[t, pl.ds(REACH + 2 * q + LEVS * (1 - 2 * half), 2)],
            send_sem=halo_send.at[q, t], recv_sem=halo_recv.at[q, t],
            device_id=(me, (lev + LEVS - 1 + 2 * half) % LEVS), device_id_type=MESH,
        )

    def slot_sums(bufs, t, q):
        rows = pl.ds(pl.multiple_of(HEAD + t * PART + q * 2 * SHARE, 16), 2 * SHARE)
        pieces = [buf[s, rows].astype(f32) for buf in bufs for s in range(TILES)]
        even = jnp.concatenate([p[:SHARE] for p in pieces], axis=0).astype(bf16)
        odd = jnp.concatenate([p[SHARE:] for p in pieces], axis=0).astype(bf16)
        first = 0 if bufs[0] is rbuf else SLOTS
        weights = chosen[:, first : first + SLOTS * len(bufs)]
        return dot(weights, jnp.concatenate([even, odd], axis=1))

    def own_rows(t, q, h):
        return pl.ds(pl.multiple_of((t * LEVS + 2 * q + h) * PITCH, 8), BLOCKS)

    def add_extras(t):
        def pair(q, carry):
            both = slot_sums((ebuf,), t, q)
            for h in range(2):
                own[own_rows(t, q, h), :] += both[:, h * CELLS : (h + 1) * CELLS]
            return carry

        lax.fori_loop(0, LEVS // 2, pair, 0)

    def gather_sum(t, half):
        bufs = (rbuf,) if t == TRACERS - 1 else (rbuf, ebuf)

        def pair(n, carry):
            q = half * 2 + n
            both = slot_sums(bufs, t, q)
            for h in range(2):
                mine = own[own_rows(t, q, h), :]
                pad[t, REACH + 2 * q + h] = (mine + both[:, h * CELLS : (h + 1) * CELLS]).astype(bf16)
            halo(t, q).start()
            return carry

        lax.fori_loop(0, 2, pair, 0)

    def remap(t):
        def chunk(g, carry):
            rows = pl.ds(pl.multiple_of(g * 16, 16), 16)
            levels = [pad[t, m, rows].astype(f32) for m in range(LEVS + 2 * REACH)]
            for l in range(LEVS):
                total = weight[l, rows] * levels[l]
                for n in range(1, TAP):
                    total = total + weight[n * LEVS + l, rows] * levels[l + n]
                turn[pl.ds(l, 16, stride=LEVS), :] = total
            for b in range(16):
                out_ref[g * 16 + b, t] = turn[b * LEVS : (b + 1) * LEVS, :].astype(bf16)
            return carry

        lax.fori_loop(0, BLOCKS // 16, chunk, 0)

    def finish(t):
        for q in range(LEVS // 2):
            halo(t, q).wait_recv()
        remap(t)

    keep_main.wait()
    for s in range(PHASES):
        wait_bytes(rbuf, s, recv_sem.at[s])
        if s == 0:
            for n in range(2, 4):
                cross(n).wait_recv()
            choose()
        if s < TRACERS - 1 or PHASES == TRACERS:
            gather_sum(s, first_half)
            gather_sum(s, 1 - first_half)
        else:
            gather_sum(TRACERS - 1, half_of(s))
        if 0 < s < TRACERS:
            finish(s - 1)
        if s == TRACERS - 2:
            add_extras(TRACERS - 1)
    finish(TRACERS - 1)
    for s in range(2, PHASES):
        wait_bytes(sbuf, s, send_sem.at[s])
    for t in range(TRACERS):
        for q in range(LEVS // 2):
            halo(t, q).wait_send()
    for n in range(4):
        for way in (1, -1):
            ring(n, way).wait_send()
        cross(n).wait_send()


def on_device(tracers, sweeps, targets, matrix_ids, self_ids, vertical):
    vmem = pl.BlockSpec(memory_space=pltpu.VMEM)
    hbm = pl.BlockSpec(memory_space=pl.ANY)
    dma = pltpu.SemaphoreType.DMA
    return pl.pallas_call(
        main_kernel,
        name="remap",
        out_shape=pltpu.VMEM((BLOCKS, TRACERS, LEVS, CELLS), bf16),
        in_specs=[hbm] * 6,
        out_specs=vmem,
        scratch_shapes=[
            pltpu.VMEM((3, BLOCKS), i32),
            pltpu.VMEM((3, 2, BLOCKS), i32),
            pltpu.SMEM((2, BLOCKS), i32),
            pltpu.VMEM((BLOCKS, ROWS, CELLS), bf16),
            pltpu.VMEM((32, CELLS, CELLS), bf16),
            pltpu.VMEM((TAP * LEVS, BLOCKS), f32),
            pltpu.VMEM((40, 128), i32),
            pltpu.SMEM((40, 128), i32),
            pltpu.VMEM((HEAD, 128), f32),
            pltpu.VMEM((8, 128), f32),
            pltpu.VMEM((SHARE * ROWS, CELLS), f32),
            pltpu.VMEM((TILES + 1, MSG, CELLS), bf16),
            pltpu.VMEM((TILES, MSG, CELLS), bf16),
            pltpu.VMEM((TILES, MSG, CELLS), bf16),
            pltpu.VMEM((ROWS * PITCH, CELLS), f32),
            pltpu.VMEM((BLOCKS, 2 * SLOTS), bf16),
            pltpu.VMEM((TRACERS, LEVS + 2 * REACH, BLOCKS, CELLS), bf16),
            pltpu.VMEM((BLOCKS, 128), f32),
            pltpu.VMEM((TAP * LEVS, BLOCKS, CELLS), f32),
            pltpu.VMEM((16 * LEVS, CELLS), f32),
            dma((7,)), dma((PHASES,)), dma((PHASES,)), dma((2, 4)), dma((2, 4)), dma((4,)), dma((4,)),
            dma((LEVS // 2, TRACERS)), dma((LEVS // 2, TRACERS)), dma((2,)),
        ],
        compiler_params=pltpu.CompilerParams(
            collective_id=0, has_side_effects=True, vmem_limit_bytes=56 * 1024 * 1024
        ),
    )(
        targets.T,
        jnp.transpose(matrix_ids, (1, 2, 0)),
        self_ids.T,
        tracers.reshape(BLOCKS, ROWS, CELLS),
        sweeps.reshape(-1, CELLS, CELLS),
        vertical.reshape(TAP * LEVS, BLOCKS),
    )


def solution(mesh):
    placed = (
        P("tile", None, "lev", None),
        P(),
        P("tile", None),
        P("tile", None, None),
        P("tile", None),
        P(None, "lev", "tile"),
    )
    return jax.shard_map(
        on_device,
        mesh=mesh,
        in_specs=placed,
        out_specs=P("tile", None, "lev", None),
        check_vma=False,
    )
```

```python
import functools

import jax
import jax.numpy as jnp
from jax import lax
from jax.experimental import pallas as pl
from jax.experimental.pallas import tpu as pltpu
from jax.sharding import PartitionSpec as P

MESH = pl.DeviceIdType.MESH
REACH = 4
XN, ZN = 4, 8
TILES = XN * ZN
BLOCKS = 256
CELLS = 128
TRACERS = 4
LEVS = 8
ROWS = TRACERS * LEVS
SHARE = 24
TAP = 2 * REACH + 1
HEAD = 16
PART = SHARE * LEVS
MSG = HEAD + TRACERS * PART
HALF = 384
PITCH = BLOCKS + 8
SLOTS = TILES * SHARE
STOPS = (4, 8, 12, 16)
PHASES = TRACERS + 1
f32, bf16, i32 = jnp.float32, jnp.bfloat16, jnp.int32


def ORDER(i):
    return jnp.where(i % 2 == 0, TILES - 2 - i // 2, i // 2)


def dot(a, b):
    return jnp.dot(a, b, preferred_element_type=f32)


def main_kernel(
    target_in, matrix_in, self_in, tracers_in, sweeps_in, vertical_in, out_ref,
    target_ref, matrix_ref, self_ref,
    tracers_ref, sweeps_ref, vertical_ref, table_made, table_ref, head, hot,
    stage, sbuf, rbuf, ebuf, own, chosen, pad, turned, weight, turn, late,
    in_sem, send_sem, recv_sem, ring_send, ring_recv, cross_send, cross_recv, halo_send, halo_recv, local_sem,
):
    me = lax.axis_index("tile")
    lev = lax.axis_index("lev")
    x, z = me // ZN, me % ZN

    def wrap(v, n):
        return jnp.where(v >= n, v - n, v)

    def tile_at(dx, dz):
        return wrap(x + dx, XN) * ZN + wrap(z + dz, ZN)

    def tile_of(k):
        return tile_at(k // ZN, k % ZN)

    moves = (
        (target_in, target_ref), (matrix_in, matrix_ref), (self_in, self_ref),
        (sweeps_in, sweeps_ref), (tracers_in, tracers_ref), (vertical_in, vertical_ref),
    )
    loads = [pltpu.make_async_copy(src, dst, in_sem.at[n]) for n, (src, dst) in enumerate(moves)]
    for load in loads:
        load.start()
    barrier = pltpu.get_barrier_semaphore()

    for dx in range(XN):
        for dz in range(ZN):
            if dx or dz:
                pl.semaphore_signal(barrier, inc=1, device_id=(tile_at(dx, dz), lev), device_id_type=MESH)
    above, below = (lev + 1) % LEVS, (lev + LEVS - 1) % LEVS
    for other in (above, below):
        pl.semaphore_signal(barrier, inc=1, device_id=(me, other), device_id_type=MESH)

    def plan():
        def over_blocks(a, b):
            return lax.dot_general(a, b.astype(bf16), (((1,), (1,)), ((), ())), preferred_element_type=f32)

        sub = lax.broadcasted_iota(i32, (40, BLOCKS), 0)
        slot = lax.broadcasted_iota(i32, (SLOTS, BLOCKS), 0)
        block = lax.broadcasted_iota(i32, (1, BLOCKS), 1).astype(f32)
        before = (
            lax.broadcasted_iota(i32, (BLOCKS, BLOCKS), 0) < lax.broadcasted_iota(i32, (BLOCKS, BLOCKS), 1)
        ).astype(f32).astype(bf16)
        base = jnp.zeros((40, 1), f32)
        line = lax.broadcasted_iota(i32, (8, BLOCKS), 0)
        total, index = None, None
        for j in range(3):
            target = target_ref[j : j + 1, :]
            owner = target >> 8
            apart = (((owner >> 3) - x) & (XN - 1)) * ZN + (((owner & (ZN - 1)) - z) & (ZN - 1))
            hits = (jnp.broadcast_to(apart, (40, BLOCKS)) == sub).astype(f32)
            earlier = dot(hits.astype(bf16), before) + base
            rank = jnp.sum(hits * earlier, axis=0, keepdims=True).astype(i32)
            base = base + jnp.sum(hits, axis=1, keepdims=True)
            extra = rank >= SHARE
            row = jnp.where(extra, TILES, apart)
            entry = jnp.where(extra, rank - SHARE, rank)
            order = jnp.where(extra, me, apart) * SHARE + entry
            taken = (jnp.broadcast_to(row, (40, BLOCKS)) == sub).astype(f32).astype(bf16)
            at_entry = (jnp.broadcast_to(entry, (32, BLOCKS)) == sub[:32]).astype(f32)
            arrival = ((target & (BLOCKS - 1)) + 1).astype(f32)
            ids = matrix_ref[j].astype(f32)
            at = (jnp.broadcast_to(order, (SLOTS, BLOCKS)) == slot).astype(f32)
            values = jnp.concatenate([at_entry * block, at_entry * ids[0:1], at_entry * ids[1:2], at_entry], axis=0)
            part = over_blocks(taken, values)
            total = part if total is None else total + part
            kind = (jnp.broadcast_to(extra.astype(i32), (8, BLOCKS)) == line).astype(f32).astype(bf16)
            part = over_blocks(kind, at * arrival)
            index = part if index is None else index + part
        table_made[...] = total.astype(i32)
        head[...] = jnp.zeros((HEAD, 128), f32)
        for m in range(SLOTS // 128):
            head[m : m + 1] = index[0:1, 128 * m : 128 * (m + 1)]
            head[8 + m : 9 + m] = index[1:2, 128 * m : 128 * (m + 1)]
        sbuf[TILES, 0:HEAD] = head[...].astype(bf16)
        hot[...] = jnp.broadcast_to((base[0:1] > SHARE).astype(f32), (8, 128))
        copy = pltpu.make_async_copy(table_made, table_ref, in_sem.at[6])
        copy.start()
        copy.wait()

    for load in loads[:3]:
        load.wait()
    plan()
    for load in loads[3:]:
        load.wait()

    def swept(block, first, second):
        half = dot(tracers_ref[block], sweeps_ref[first]).astype(bf16)
        return dot(half, sweeps_ref[16 + second])

    def build(k):
        for e in range(SHARE):
            stage[pl.ds(e, ROWS, stride=SHARE), :] = swept(
                table_ref[k, e] & (BLOCKS - 1), table_ref[k, 32 + e] & 15, table_ref[k, 64 + e] & 15
            )
        for t in range(TRACERS):
            sbuf[k, HEAD + t * PART : HEAD + (t + 1) * PART] = stage[t * PART : (t + 1) * PART, :].astype(bf16)

    first_half = lev % 2

    def half_of(s):
        return first_half if s == TRACERS - 1 else 1 - first_half

    def span(s):
        if s < TRACERS - 1 or PHASES == TRACERS:
            return pl.ds(HEAD + s * PART, PART)
        start = HEAD + (TRACERS - 1) * PART + half_of(s) * (PART // 2)
        return pl.ds(pl.multiple_of(start, 16), PART // 2)

    def send(t, k):
        return pltpu.make_async_remote_copy(
            src_ref=sbuf.at[k, span(t)], dst_ref=rbuf.at[k, span(t)],
            send_sem=send_sem.at[t], recv_sem=recv_sem.at[t],
            device_id=(tile_of(k), lev), device_id_type=MESH,
        )

    def wait_bytes(buf, t, sem):
        ref = buf.at[pl.ds(1, TILES - 1), span(t)]
        pltpu.make_async_copy(ref, ref, sem).wait()

    def ring(j, way):
        item = x * ZN + (z - way * j + ZN) % ZN
        rows = pl.ds(0, MSG) if j < 3 else (pl.ds(0, HALF) if way > 0 else pl.ds(HALF, MSG - HALF))
        d = 0 if way > 0 else 1
        return pltpu.make_async_remote_copy(
            src_ref=sbuf.at[TILES, rows] if j == 0 else ebuf.at[item, rows],
            dst_ref=ebuf.at[item, rows],
            send_sem=ring_send.at[d, j], recv_sem=ring_recv.at[d, j],
            device_id=(tile_at(0, way % ZN), lev), device_id_type=MESH,
        )

    def cross(n):
        way = 1 if n % 2 == 0 else -1
        first = (x if n < 2 else (x - way + XN) % XN) * ZN
        group = pl.ds(first, ZN) if n < 2 else pl.ds(first if way > 0 else first + ZN // 2, ZN // 2)
        return pltpu.make_async_remote_copy(
            src_ref=ebuf.at[group], dst_ref=ebuf.at[group],
            send_sem=cross_send.at[n], recv_sem=cross_recv.at[n],
            device_id=(tile_at(way % XN, 0), lev), device_id_type=MESH,
        )

    def keep(src, dst, i):
        return pltpu.make_async_copy(src, dst, local_sem.at[i])

    keep_extra = keep(sbuf.at[TILES], ebuf.at[me], 0)
    keep_main = keep(sbuf.at[0], rbuf.at[0], 1)
    def partner(p):
        side = jnp.where(p % 2 == 0, p // 8 + 1, ZN - 1 - p // 8)
        side = jnp.where(lev % 2 == 0, side, ZN - side)
        dz = jnp.where(p < 24, side, jnp.where(p < 28, ZN // 2, 0))
        dx = jnp.where(p < 24, (p % 8) // 2, jnp.where(p < 28, p - 24, p - 27))
        return dx * ZN + dz

    stops = STOPS

    def step(i, carry):
        k = jnp.where(i == 0, TILES, jnp.where(i == TILES, 0, partner(i - 1)))
        build(k)

        @pl.when(i == 0)
        def _():
            pl.semaphore_wait(barrier, TILES + 1)
            ring(0, 1).start()
            ring(0, -1).start()
            keep_extra.start()

        @pl.when(jnp.logical_and(i > 0, i < TILES))
        def _():
            send(0, k).start()

        for j, stop in enumerate(stops):
            @pl.when(i == stop)
            def _():
                for way in (1, -1):
                    ring(j, way).wait_recv()
                if j < 3:
                    for way in (1, -1):
                        ring(j + 1, way).start()
                else:
                    keep_extra.wait()

        return carry

    lax.fori_loop(0, TILES + 1, step, 0)
    keep_main.start()

    def send_phase(t):
        def one(i, carry):
            send(t, partner(ORDER(i))).start()
            return carry

        lax.fori_loop(0, TILES - 1, one, 0)

    send_phase(1)
    cross(0).start()
    cross(1).start()

    def own_step(g, carry):
        for u in range(8):
            b = g * 8 + u
            own[pl.ds(b, ROWS, stride=PITCH), :] = swept(b, self_ref[0, b] & 15, self_ref[1, b] & 15)
        return carry

    lax.fori_loop(0, BLOCKS // 8, own_step, 0)
    wait_bytes(sbuf, 0, send_sem.at[0])
    send_phase(2)

    tap_row = lax.broadcasted_iota(i32, (TAP * LEVS, BLOCKS), 0)
    source = lev * LEVS + tap_row % LEVS + tap_row // LEVS - REACH
    plain = vertical_ref[...] + jnp.where(tap_row // LEVS == REACH, 1.0, 0.0)
    turned[:, : TAP * LEVS] = jnp.where(jnp.logical_and(source >= 0, source < LEVS * LEVS), plain, 0.0).T

    def spread(g, carry):
        rows = pl.ds(pl.multiple_of(g * 8, 8), 8)
        columns = turned[rows, :]
        for n in range(TAP * LEVS):
            weight[n, rows] = jnp.broadcast_to(columns[:, n : n + 1], (8, CELLS))
        return carry

    lax.fori_loop(0, BLOCKS // 8, spread, 0)
    for n in range(2):
        cross(n).wait_recv()
    for n in range(2, 4):
        cross(n).start()
    wait_bytes(sbuf, 1, send_sem.at[1])
    send_phase(3)
    send_phase(4)

    def choose():
        lane = lax.broadcasted_iota(i32, (8, 128), 0) * 128 + lax.broadcasted_iota(i32, (8, 128), 1)

        def add(s, sums):
            tile = ebuf[s, 0:HEAD].astype(f32)
            k = ((x - s // ZN + XN) % XN) * ZN + (z - s % ZN + ZN) % ZN
            mine = jnp.logical_and(lane >= k * SHARE, lane < (k + 1) * SHARE)
            return sums[0] + jnp.where(mine, tile[0:8], 0.0), sums[1] + tile[8:16]

        none = jnp.zeros((8, 128), f32)
        main, extra = lax.fori_loop(0, TILES, add, (none, none))
        extra = extra * hot[...]
        block = lax.broadcasted_iota(i32, (BLOCKS, 128), 0).astype(f32) + 1.0
        for first, tile in ((0, main), (SLOTS, extra)):
            for m in range(SLOTS // 128):
                hit = (jnp.broadcast_to(tile[m : m + 1], (BLOCKS, 128)) == block).astype(f32)
                chosen[:, first + 128 * m : first + 128 * (m + 1)] = hit.astype(bf16)

    def halo(t, q):
        half = q // 2
        return pltpu.make_async_remote_copy(
            src_ref=pad.at[t, pl.ds(REACH + 2 * q, 2)],
            dst_ref=pad.at[t, pl.ds(REACH + 2 * q + LEVS * (1 - 2 * half), 2)],
            send_sem=halo_send.at[q, t], recv_sem=halo_recv.at[q, t],
            device_id=(me, (lev + LEVS - 1 + 2 * half) % LEVS), device_id_type=MESH,
        )

    def slot_sums(bufs, t, q):
        rows = pl.ds(pl.multiple_of(HEAD + t * PART + q * 2 * SHARE, 16), 2 * SHARE)
        pieces = [buf[s, rows].astype(f32) for buf in bufs for s in range(TILES)]
        even = jnp.concatenate([p[:SHARE] for p in pieces], axis=0).astype(bf16)
        odd = jnp.concatenate([p[SHARE:] for p in pieces], axis=0).astype(bf16)
        first = 0 if bufs[0] is rbuf else SLOTS
        weights = chosen[:, first : first + SLOTS * len(bufs)]
        return dot(weights, jnp.concatenate([even, odd], axis=1))

    def own_rows(t, q, h):
        return pl.ds(pl.multiple_of((t * LEVS + 2 * q + h) * PITCH, 8), BLOCKS)

    def add_extras(t):
        def pair(q, carry):
            both = slot_sums((ebuf,), t, q)
            for h in range(2):
                own[own_rows(t, q, h), :] += both[:, h * CELLS : (h + 1) * CELLS]
            return carry

        lax.fori_loop(0, LEVS // 2, pair, 0)

    def gather_sum(t, half):
        bufs = (rbuf,) if t == TRACERS - 1 else (rbuf, ebuf)

        def pair(n, carry):
            q = half * 2 + n
            both = slot_sums(bufs, t, q)
            for h in range(2):
                mine = own[own_rows(t, q, h), :]
                pad[t, REACH + 2 * q + h] = (mine + both[:, h * CELLS : (h + 1) * CELLS]).astype(bf16)
            halo(t, q).start()
            return carry

        lax.fori_loop(0, 2, pair, 0)

    def remap(t):
        def chunk(g, carry):
            rows = pl.ds(pl.multiple_of(g * 16, 16), 16)
            levels = [pad[t, m, rows].astype(f32) for m in range(LEVS + 2 * REACH)]
            for l in range(LEVS):
                total = weight[l, rows] * levels[l]
                for n in range(1, TAP):
                    total = total + weight[n * LEVS + l, rows] * levels[l + n]
                turn[pl.ds(l, 16, stride=LEVS), :] = total
            for b in range(16):
                out_ref[g * 16 + b, t] = turn[b * LEVS : (b + 1) * LEVS, :].astype(bf16)
            return carry

        lax.fori_loop(0, BLOCKS // 16, chunk, 0)

    def remap_half(half, last):
        t = TRACERS - 1

        def chunk(g, carry):
            rows = pl.ds(pl.multiple_of(g * 16, 16), 16)
            levels = [pad[t, REACH * half + m, rows].astype(f32) for m in range(REACH + 2 * REACH)]
            for l in range(REACH):
                total = weight[REACH * half + l, rows] * levels[l]
                for n in range(1, TAP):
                    total = total + weight[n * LEVS + REACH * half + l, rows] * levels[l + n]
                late[pl.ds(g * 16 * LEVS + REACH * half + l, 16, stride=LEVS), :] = total
            if last:
                for b in range(16):
                    tile = late[pl.ds(pl.multiple_of((g * 16 + b) * LEVS, 8), LEVS), :]
                    out_ref[g * 16 + b, t] = tile.astype(bf16)
            return carry

        lax.fori_loop(0, BLOCKS // 16, chunk, 0)

    def finish_last():
        for half, last in ((first_half, False), (1 - first_half, True)):
            for n in range(2):
                halo(TRACERS - 1, 2 * (1 - half) + n).wait_recv()
            remap_half(half, last)

    def finish(t):
        for q in range(LEVS // 2):
            halo(t, q).wait_recv()
        remap(t)

    keep_main.wait()
    for s in range(PHASES):
        wait_bytes(rbuf, s, recv_sem.at[s])
        if s == 0:
            for n in range(2, 4):
                cross(n).wait_recv()
            choose()
        if s < TRACERS - 1 or PHASES == TRACERS:
            gather_sum(s, first_half)
            gather_sum(s, 1 - first_half)
        else:
            gather_sum(TRACERS - 1, half_of(s))
        if 0 < s < TRACERS:
            finish(s - 1)
        if s == TRACERS - 2:
            add_extras(TRACERS - 1)
    finish_last()
    for s in range(2, PHASES):
        wait_bytes(sbuf, s, send_sem.at[s])
    for t in range(TRACERS):
        for q in range(LEVS // 2):
            halo(t, q).wait_send()
    for n in range(4):
        for way in (1, -1):
            ring(n, way).wait_send()
        cross(n).wait_send()


def on_device(tracers, sweeps, targets, matrix_ids, self_ids, vertical):
    vmem = pl.BlockSpec(memory_space=pltpu.VMEM)
    hbm = pl.BlockSpec(memory_space=pl.ANY)
    dma = pltpu.SemaphoreType.DMA
    return pl.pallas_call(
        main_kernel,
        name="remap",
        out_shape=pltpu.VMEM((BLOCKS, TRACERS, LEVS, CELLS), bf16),
        in_specs=[hbm] * 6,
        out_specs=vmem,
        scratch_shapes=[
            pltpu.VMEM((3, BLOCKS), i32),
            pltpu.VMEM((3, 2, BLOCKS), i32),
            pltpu.SMEM((2, BLOCKS), i32),
            pltpu.VMEM((BLOCKS, ROWS, CELLS), bf16),
            pltpu.VMEM((32, CELLS, CELLS), bf16),
            pltpu.VMEM((TAP * LEVS, BLOCKS), f32),
            pltpu.VMEM((40, 128), i32),
            pltpu.SMEM((40, 128), i32),
            pltpu.VMEM((HEAD, 128), f32),
            pltpu.VMEM((8, 128), f32),
            pltpu.VMEM((SHARE * ROWS, CELLS), f32),
            pltpu.VMEM((TILES + 1, MSG, CELLS), bf16),
            pltpu.VMEM((TILES, MSG, CELLS), bf16),
            pltpu.VMEM((TILES, MSG, CELLS), bf16),
            pltpu.VMEM((ROWS * PITCH, CELLS), f32),
            pltpu.VMEM((BLOCKS, 2 * SLOTS), bf16),
            pltpu.VMEM((TRACERS, LEVS + 2 * REACH, BLOCKS, CELLS), bf16),
            pltpu.VMEM((BLOCKS, 128), f32),
            pltpu.VMEM((TAP * LEVS, BLOCKS, CELLS), f32),
            pltpu.VMEM((16 * LEVS, CELLS), f32),
            pltpu.VMEM((BLOCKS * LEVS, CELLS), f32),
            dma((7,)), dma((PHASES,)), dma((PHASES,)), dma((2, 4)), dma((2, 4)), dma((4,)), dma((4,)),
            dma((LEVS // 2, TRACERS)), dma((LEVS // 2, TRACERS)), dma((2,)),
        ],
        compiler_params=pltpu.CompilerParams(
            collective_id=0, has_side_effects=True, vmem_limit_bytes=56 * 1024 * 1024
        ),
    )(
        targets.T,
        jnp.transpose(matrix_ids, (1, 2, 0)),
        self_ids.T,
        tracers.reshape(BLOCKS, ROWS, CELLS),
        sweeps.reshape(-1, CELLS, CELLS),
        vertical.reshape(TAP * LEVS, BLOCKS),
    )


def solution(mesh):
    placed = (
        P("tile", None, "lev", None),
        P(),
        P("tile", None),
        P("tile", None, None),
        P("tile", None),
        P(None, "lev", "tile"),
    )
    return jax.shard_map(
        on_device,
        mesh=mesh,
        in_specs=placed,
        out_specs=P("tile", None, "lev", None),
        check_vma=False,
    )
```
